512 devices in a mesh: tm: 16 (over y, core), nin: 8 (over z), nout: 4 (over x).
Axes of the slice: x: 4, y: 8, z: 8, core: 2. Of those that a mesh axis runs over, the one named last changes fastest.
Arguments:
- spikes: int32 [4096, 2048], P('tm', 'nin'), may hold values 0 or 1
- exposure: int32 [4096], P('tm'), may hold values from 1 to 8
- weights: bfloat16 [16384, 2048], P('nin', 'nout'), may hold values from -0.375 to 0.375
- direction: float32 [16384, 2048], P(('nin', 'tm'), 'nout'), may hold values from -6 to 6
- residual: float32 [16384, 2048], P(('nin', 'tm'), 'nout'), may hold values from -0.75 to 0.75
- iterate: float32 [16384, 2048], P(('nin', 'tm'), 'nout'), may hold values from -1.8 to 1.8
Outputs:
- new_iterate: float32 [16384, 2048], P(('nin', 'tm'), 'nout')
- new_residual: float32 [16384, 2048], P(('nin', 'tm'), 'nout')
- new_direction: float32 [16384, 2048], P(('nin', 'tm'), 'nout')
The draws below stay inside these ranges and needn't reach their ends.
All inputs are finite; a program needn't handle non-finite values. No bound on the sum of `spikes` on one device may be relied on, other than what follows from the above.
Results may differ from the reference program's by a relative error of at most 0.015.
Values may be sent and summed in bfloat16 or wider, within the bound.
A program may use at most 64 MiB of HBM per device.

```python
import math
import jax
import jax.numpy as jnp
from jax import lax

NEURONS = 2048
BASES = 8
HISTORY = 128
BIN_DEV = 256
FEATURES = 16384
BINS = 4096


def plant(values, own_key, smallest, largest):
    shape = values.shape
    spot = [jax.random.randint(jax.random.fold_in(own_key, axis), (), 0, shape[axis]) for axis in range(len(shape))]
    values = values.at[tuple(spot)].set(smallest)
    longest = shape.index(max(shape))
    spot[longest] = (spot[longest] + 1) % shape[longest]
    return values.at[tuple(spot)].set(largest)


def block_scale(key, dims, pieces, least, top_value):
    def one(dim, blocks):
        heights = jax.random.uniform(jax.random.fold_in(jax.random.fold_in(key, 6), dim), (blocks,), jnp.float32, least / len(pieces), top_value / len(pieces))
        return jnp.repeat(jnp.exp(heights), dims[dim] // blocks).reshape((-1,) + (1,) * (len(dims) - dim - 1))

    gain = one(*pieces[0])
    for cut in pieces[1:]:
        gain = gain * one(*cut)
    return gain


def gaussian(key, extent, width, reach, split=(), kind=jnp.bfloat16):
    array = width * jax.random.normal(key, extent, jnp.float32)
    if split:
        array = array * block_scale(key, extent, split, -0.22, 0.18)
    return jnp.clip(array, -reach, reach).astype(kind)


def setup_inputs(seed: int = 0) -> dict:
    arg_keys = jax.random.split(jax.random.key(seed), 7)
    return {
        "spikes": plant((jax.random.randint(arg_keys[0], (BINS, NEURONS), 0, 12) < 1).astype(jnp.int32), jax.random.fold_in(arg_keys[0], 1), 0, 1),
        "exposure": plant(jax.random.randint(arg_keys[1], (BINS,), 1, 9), jax.random.fold_in(arg_keys[1], 1), 1, 8).astype(jnp.int32),
        "weights": gaussian(arg_keys[2], (FEATURES, NEURONS), (FEATURES // 64) ** -0.5, 0.375, ((0, 8), (1, 4))),
        "direction": gaussian(arg_keys[3], (FEATURES, NEURONS), 1.0, 6.0, ((0, 128), (1, 4)), jnp.float32),
        "residual": gaussian(arg_keys[4], (FEATURES, NEURONS), 0.125, 0.75, ((0, 128), (1, 4)), jnp.float32),
        "iterate": gaussian(arg_keys[5], (FEATURES, NEURONS), 0.3, 1.8, ((0, 128), (1, 4)), jnp.float32),
    }


RIDGE_WEIGHT = 0.05
NORM_EPS = 1e-6


def basis_table(history, bases_count):
    lag_values = jnp.arange(1, history + 1, dtype=jnp.float32)
    warped = jnp.log(lag_values + 1.0)
    log_low = math.log(2.0)
    log_high = math.log(history + 1.0)
    spacing = (log_high - log_low) / (bases_count - 1)
    centers = log_low + spacing * jnp.arange(bases_count, dtype=jnp.float32)
    phases = (warped[:, None] - centers[None, :]) * (math.pi / (2.0 * spacing))
    phases = jnp.clip(phases, -math.pi, math.pi)
    bump_values = 0.5 * (1.0 + jnp.cos(phases))
    bump_values = bump_values / jnp.sum(bump_values, axis=0, keepdims=True)
    return bump_values.astype(jnp.bfloat16)


def reference(spikes, exposure, weights, direction, residual, iterate):
    basis_rows = basis_table(HISTORY, BASES)
    out_index = jnp.arange(BIN_DEV, dtype=jnp.int32)[:, None]
    in_index = jnp.arange(BIN_DEV + HISTORY, dtype=jnp.int32)[None, :]
    lag_index = out_index + HISTORY - in_index
    is_valid = (lag_index >= 1) & (lag_index <= HISTORY)
    take_index = jnp.clip(lag_index - 1, 0, HISTORY - 1).astype(jnp.int32)
    kernel = jnp.where(is_valid[None], jnp.take(basis_rows.T, take_index, axis=1), jnp.zeros((), jnp.bfloat16))
    kernel_wide = kernel.astype(jnp.float32)
    padded = jnp.concatenate([jnp.zeros((HISTORY, NEURONS), jnp.float32), spikes.astype(jnp.float32)], axis=0)
    direction_low = direction.astype(jnp.bfloat16)
    block_count = BINS // BIN_DEV

    def one_block(block, running):
        begin_row = (block * BIN_DEV).astype(jnp.int32)
        window = lax.dynamic_slice_in_dim(padded, begin_row, BIN_DEV + HISTORY, 0)
        convolved = jnp.einsum("bim,mn->bin", kernel_wide, window)
        features = jnp.transpose(convolved, (1, 2, 0)).reshape(BIN_DEV, FEATURES).astype(jnp.bfloat16)
        predictor = jnp.dot(features, weights, preferred_element_type=jnp.float32)
        tick_scale = lax.dynamic_slice_in_dim(exposure, begin_row, BIN_DEV, 0).astype(jnp.float32) / 8.0
        along_dir = jnp.dot(features, direction_low, preferred_element_type=jnp.float32)
        weighted = ((tick_scale[:, None] * jnp.exp(predictor)) * along_dir).astype(jnp.bfloat16)
        partial_sum = jnp.dot(features.T, weighted, preferred_element_type=jnp.float32).astype(jnp.bfloat16)
        return running + partial_sum.astype(jnp.float32)

    gram = lax.fori_loop(0, block_count, one_block, jnp.zeros((FEATURES, NEURONS), jnp.float32))
    curvature_prod = gram / BINS + RIDGE_WEIGHT * direction
    old_norm = jnp.sum(residual * residual, axis=0)
    curvature = jnp.sum(direction * curvature_prod, axis=0)
    step_size = old_norm / curvature
    new_iterate = iterate + step_size[None, :] * direction
    new_residual = residual - step_size[None, :] * curvature_prod
    new_norm = jnp.sum(new_residual * new_residual, axis=0)
    new_direction = new_residual + (new_norm / (old_norm + NORM_EPS))[None, :] * direction
    return (new_iterate, new_residual, new_direction)
```

```python
import functools
import math

import jax
import jax.numpy as jnp
import numpy as np
from jax import lax
from jax.experimental import pallas as pl
from jax.experimental.pallas import tpu as pltpu
from jax.sharding import PartitionSpec as P

BASES = 8
HISTORY = 128
RIDGE_WEIGHT = 0.05
NORM_EPS = 1e-06
MESH = pl.DeviceIdType.MESH
F32 = jnp.float32
BF16 = jnp.bfloat16

TM = 16
NIN = 8
GROUP = 4
BINS = 1024
OWN = 256
NEUR = 256
COLS = 128
FEAT = NEUR * BASES
SLOT = NEUR // TM


def basis_table():
    lag_values = np.arange(1, HISTORY + 1, dtype=np.float32)
    warped = np.log(lag_values + np.float32(1.0))
    log_low = math.log(2.0)
    log_high = math.log(HISTORY + 1.0)
    spacing = (log_high - log_low) / (BASES - 1)
    centers = np.float32(log_low) + np.float32(spacing) * np.arange(BASES, dtype=np.float32)
    phases = (warped[:, None] - centers[None, :]) * np.float32(math.pi / (2.0 * spacing))
    phases = np.clip(phases, np.float32(-math.pi), np.float32(math.pi))
    bumps = np.float32(0.5) * (np.float32(1.0) + np.cos(phases))
    bumps = bumps / np.sum(bumps, axis=0, keepdims=True)
    return bumps.astype(np.float32)


def lag_table():
    basis = basis_table()
    lag = np.arange(HISTORY)[:, None] + HISTORY - np.arange(2 * HISTORY)[None, :]
    valid = (lag >= 1) & (lag <= HISTORY)
    table = np.where(valid[None], basis.T[:, np.clip(lag - 1, 0, HISTORY - 1)], np.float32(0.0))
    return table.reshape(BASES * HISTORY, 2 * HISTORY)


def kernel(
    exposure_ref, spikes_hbm, weights_hbm, direction_hbm, residual_hbm, iterate_hbm, lag_hbm, lag_t_hbm,
    iterate_out, residual_out, direction_out,
    spikes_in, lag, lag_t, d32, r32, it32, w16, w32, wp, spk, spk_t, x, xt,
    d_send, d_all, p_own, p_send, p_recv, a_own, a_send, a_recv, wt_all, g_send, g_recv, g_nat,
    ticks, ticks_t, nd_send, nd_recv, cv_send, cv_recv, c2_send, c2_recv, nn_send, nn_recv, nz_send, nz_recv,
    load_sem, spk_sem, halo_sem, tick_sem, d_sem, p_sem, a_sem, wt_sem, g_sem, nd_sem, cv_sem, c2_sem, nn_sem, nz_sem,
):
    me = lax.axis_index("tm")
    z = lax.axis_index("nin")
    xo = lax.axis_index("nout")
    team = me // GROUP
    part = lax.rem(me, GROUP)

    def tm_peer(step):
        return lax.rem(me + step, TM)

    def z_peer(step):
        return lax.rem(z + step, NIN)

    def team_peer(step):
        return team * GROUP + lax.rem(part + step, GROUP)

    def remote(src, dst, sems, slot, tm_index, z_index):
        return pltpu.make_async_remote_copy(
            src_ref=src, dst_ref=dst, send_sem=sems.at[0, slot], recv_sem=sems.at[1, slot],
            device_id=(tm_index, z_index, xo), device_id_type=MESH,
        )

    def each(first, last, body):
        def run(step, carry):
            body(step)
            return carry

        lax.fori_loop(first, last, run, 0)

    loads = [
        pltpu.make_async_copy(spikes_hbm, spikes_in, load_sem.at[0]),
        pltpu.make_async_copy(lag_hbm, lag, load_sem.at[1]),
        pltpu.make_async_copy(lag_t_hbm, lag_t, load_sem.at[2]),
        pltpu.make_async_copy(
            weights_hbm.at[:, pl.ds(pl.multiple_of(part * COLS, COLS), COLS)], w16, load_sem.at[3]
        ),
    ]
    blocks = [
        [
            pltpu.make_async_copy(source.at[:, k * COLS : (k + 1) * COLS], target.at[k], load_sem.at[4 + 4 * n + k])
            for k in range(GROUP)
        ]
        for n, (source, target) in enumerate(((direction_hbm, d32), (residual_hbm, r32), (iterate_hbm, it32)))
    ]
    for copy in blocks[0] + loads[:1]:
        copy.start()
    for copy in loads[1:] + blocks[1] + blocks[2]:
        copy.start()

    barrier = pltpu.get_barrier_semaphore()

    def greet_tm(step):
        pl.semaphore_signal(barrier, inc=1, device_id=(tm_peer(step), z, xo), device_id_type=MESH)

    def greet_z(step):
        pl.semaphore_signal(barrier, inc=1, device_id=(me, z_peer(step), xo), device_id_type=MESH)

    each(1, TM, greet_tm)
    each(1, NIN, greet_z)

    for copy in blocks[0]:
        copy.wait()
    for k in range(GROUP):
        for b in range(BASES):
            d_send[k, b] = d32[k, pl.ds(b, SLOT, stride=BASES), :].astype(BF16)
    loads[0].wait()
    own_rows = pl.ds(pl.multiple_of(HISTORY + part * OWN, HISTORY), OWN)
    spk[own_rows, :] = spikes_in[...].astype(F32).astype(BF16)
    ticks[part, 0:2, :] = exposure_ref[...].astype(F32) / 8.0
    ticks[part, 2:8, :] = jnp.zeros((6, COLS), F32)
    pl.semaphore_wait(barrier, TM - 1 + NIN - 1)

    def spikes_copy(step):
        return remote(spk.at[own_rows], spk.at[own_rows], spk_sem, step, team_peer(step), z)

    def spikes_arrival(step):
        rows = pl.ds(pl.multiple_of(HISTORY + lax.rem(part + GROUP - step, GROUP) * OWN, HISTORY), OWN)
        return remote(spk.at[rows], spk.at[rows], spk_sem, step, team_peer(step), z)

    def halo_copy(k):
        return remote(
            spk.at[BINS : BINS + HISTORY], spk.at[0:HISTORY], halo_sem, k, lax.rem((team + 1) * GROUP + k, TM), z
        )

    def tick_copy(step):
        return remote(ticks.at[part], ticks.at[part], tick_sem, step, team_peer(step), z)

    def tick_arrival(step):
        slot = lax.rem(part + GROUP - step, GROUP)
        return remote(ticks.at[slot], ticks.at[slot], tick_sem, step, team_peer(step), z)

    d_rows = pl.ds(pl.multiple_of(me * SLOT, SLOT), SLOT)

    def direction_copy(step):
        peer = tm_peer(step)
        return remote(d_send.at[lax.rem(peer, GROUP)], d_all.at[:, d_rows, :], d_sem, step, peer, z)

    def direction_arrival(step):
        rows = pl.ds(pl.multiple_of(tm_peer(TM - step) * SLOT, SLOT), SLOT)
        return remote(d_send.at[0], d_all.at[:, rows, :], d_sem, step, tm_peer(step), z)

    sends_halo = jnp.logical_and(part == GROUP - 1, team < TM // GROUP - 1)

    each(1, GROUP, lambda step: spikes_copy(step).start())

    @pl.when(sends_halo)
    def _():
        each(0, GROUP, lambda k: halo_copy(k).start())

    each(1, TM, lambda step: direction_copy(step).start())
    each(1, GROUP, lambda step: tick_copy(step).start())
    d_all[:, d_rows, :] = d_send[part]

    for copy in blocks[1]:
        copy.wait()
    for k in range(GROUP):
        nd_send[k : k + 1, :] = jnp.sum(r32[k] * r32[k], axis=0, keepdims=True)
        nd_send[GROUP + k : GROUP + k + 1, :] = jnp.sum(d32[k] * d32[k], axis=0, keepdims=True)

    def nd_copy(step):
        return remote(nd_send, nd_recv.at[step], nd_sem, step, tm_peer(step), z)

    each(1, TM, lambda step: nd_copy(step).start())

    loads[3].wait()
    w32[...] = w16[...].astype(F32)
    for b in range(BASES):
        wp[b * NEUR : (b + 1) * NEUR, :] = w32[pl.ds(b, NEUR, stride=BASES), :].astype(BF16)
    loads[1].wait()
    loads[2].wait()

    @pl.when(team == 0)
    def _():
        spk[0:HISTORY, :] = jnp.zeros((HISTORY, NEUR), BF16)

    @pl.when(team > 0)
    def _():
        pltpu.make_async_remote_copy(
            src_ref=spk.at[0:HISTORY], dst_ref=spk.at[0:HISTORY], send_sem=halo_sem.at[0, part],
            recv_sem=halo_sem.at[1, part], device_id=(me, z, xo), device_id_type=MESH,
        ).wait_recv()

    each(1, GROUP, lambda step: spikes_arrival(step).wait_recv())

    for n in range(9):
        spk_t[:, n * HISTORY : (n + 1) * HISTORY] = spk[n * HISTORY : (n + 1) * HISTORY, :].astype(F32).T.astype(BF16)

    def features(block):
        rows = pl.ds(pl.multiple_of(block * HISTORY, HISTORY), HISTORY)
        window = pl.ds(pl.multiple_of(block * HISTORY, HISTORY), 2 * HISTORY)
        made = jnp.dot(lag[...], spk[window, :], preferred_element_type=F32)
        for b in range(BASES):
            x[rows, b * NEUR : (b + 1) * NEUR] = made[b * HISTORY : (b + 1) * HISTORY].astype(BF16)
        made_t = jnp.dot(spk_t[:, window], lag_t[...], preferred_element_type=F32)
        for b in range(BASES):
            piece = made_t[:, b * HISTORY : (b + 1) * HISTORY].astype(BF16)
            xt[:, b, :, rows] = piece.reshape(TM, SLOT, HISTORY)

    each(0, BINS // HISTORY, features)

    def predictor(half):
        rows = pl.ds(pl.multiple_of(half * 512, 512), 512)
        made = jnp.dot(x[rows, :], wp[...], preferred_element_type=F32).reshape(NIN, 64, COLS)
        p_own[half] = made
        p_send[half] = made.astype(BF16)

    each(0, 2, predictor)

    def predictor_copy(step):
        return remote(p_send.at[:, z_peer(step)], p_recv.at[:, step], p_sem, step, me, z_peer(step))

    each(1, NIN, lambda step: predictor_copy(step).start())

    each(1, TM, lambda step: direction_arrival(step).wait_recv())

    def along_copy(half, step):
        return remote(a_send.at[half, z_peer(step)], a_recv.at[half, step], a_sem, half * NIN + step, me, z_peer(step))

    def along(half):
        rows = pl.ds(pl.multiple_of(half * 512, 512), 512)
        made = jnp.dot(x[rows, :], d_all[...].reshape(FEAT, COLS), preferred_element_type=F32).reshape(NIN, 64, COLS)
        a_own[half] = made
        a_send[half] = made.astype(BF16)
        each(1, NIN, lambda step: along_copy(half, step).start())

    each(0, 2, along)

    each(1, GROUP, lambda step: tick_arrival(step).wait_recv())
    table = jnp.concatenate([ticks[k, 0:2, :] for k in range(GROUP)] + [jnp.zeros((COLS - 8, COLS), F32)], axis=0)
    ticks_t[...] = table.T
    tick_rows = ticks_t[pl.ds(pl.multiple_of(lax.rem(z, 2) * 64, 64), 64), :]
    lane = lax.broadcasted_iota(jnp.int32, (64, COLS), 1)

    each(1, TM, lambda step: nd_copy(step).wait_recv())
    cv_send[0:8, :] = nd_send[...] + jnp.sum(nd_recv[1:TM], axis=0)

    each(1, NIN, lambda step: predictor_copy(step).wait_recv())
    curvature_part = jnp.zeros((1, COLS), F32)
    for half in range(2):
        each(1, NIN, lambda step: along_copy(half, step).wait_recv())
        p_sum = p_own[half, z]
        a_sum = a_own[half, z]
        for step in range(1, NIN):
            p_sum += p_recv[half, step].astype(F32)
            a_sum += a_recv[half, step].astype(F32)
        scale = jnp.sum(jnp.where(lane == half * 4 + z // 2, tick_rows, 0.0), axis=1, keepdims=True)
        weighted = ((scale * jnp.exp(p_sum)) * a_sum).astype(BF16)
        wt_all[half, z] = weighted
        each(
            1, NIN,
            lambda step: remote(
                wt_all.at[half, z], wt_all.at[half, z], wt_sem, half * NIN + step, me, z_peer(step)
            ).start(),
        )
        curvature_part += jnp.sum(weighted.astype(F32) * a_sum, axis=0, keepdims=True)
    cv_send[8:16, :] = jnp.concatenate([curvature_part, jnp.zeros((7, COLS), F32)], axis=0)

    def cv_copy(step):
        return remote(cv_send, cv_recv.at[step], cv_sem, step, me, z_peer(step))

    each(1, NIN, lambda step: cv_copy(step).start())

    def weighted_arrival(half, step):
        slot = z_peer(NIN - step)
        return remote(wt_all.at[half, slot], wt_all.at[half, slot], wt_sem, half * NIN + step, me, z_peer(step))

    for half in range(2):
        each(1, NIN, lambda step: weighted_arrival(half, step).wait_recv())

    def gram_copy(step):
        return remote(g_send.at[tm_peer(step)], g_recv.at[me], g_sem, step, tm_peer(step), z)

    def gram_arrival(step):
        return remote(g_send.at[0], g_recv.at[tm_peer(TM - step)], g_sem, step, tm_peer(step), z)

    def gram(slots):
        rows = pl.ds(slots * 4, 4)
        made = jnp.dot(
            xt[rows].reshape(4 * SLOT * BASES, BINS), wt_all[...].reshape(BINS, COLS), preferred_element_type=F32
        )
        g_send[rows] = made.astype(BF16).reshape(4, SLOT * BASES, COLS)

    each(0, 4, gram)
    each(1, TM, lambda step: gram_copy(step).start())
    g_recv[me] = g_send[me]

    each(1, NIN, lambda step: cv_copy(step).wait_recv())
    cv_sum = cv_send[...] + jnp.sum(cv_recv[1:NIN], axis=0)
    old_norm = cv_sum[0:4, :]
    c2_send[...] = cv_sum[8:16, :]
    c2_recv[me] = cv_sum[8:16, :]

    def c2_copy(step):
        return remote(c2_send, c2_recv.at[me], c2_sem, step, tm_peer(step), z)

    def c2_arrival(step):
        return remote(c2_send, c2_recv.at[tm_peer(TM - step)], c2_sem, step, tm_peer(step), z)

    each(1, TM, lambda step: c2_copy(step).start())
    each(1, TM, lambda step: c2_arrival(step).wait_recv())
    for copy in blocks[2]:
        copy.wait()
    step_sizes = []
    for k in range(GROUP):
        total = c2_recv[k, 0:1, :]
        for t in range(1, TM // GROUP):
            total += c2_recv[t * GROUP + k, 0:1, :]
        curvature = total / (BINS * (TM // GROUP)) + RIDGE_WEIGHT * cv_sum[4 + k : 5 + k, :]
        step_size = old_norm[k : k + 1, :] / curvature
        step_sizes.append(step_size)
        iterate_out[:, k * COLS : (k + 1) * COLS] = it32[k] + step_size * d32[k]

    each(1, TM, lambda step: gram_arrival(step).wait_recv())
    nn_send[4:8, :] = jnp.zeros((4, COLS), F32)
    for k in range(GROUP):
        total = g_recv[k].astype(F32)
        for t in range(1, TM // GROUP):
            total += g_recv[t * GROUP + k].astype(F32)
        for b in range(BASES):
            g_nat[k, pl.ds(b, SLOT, stride=BASES), :] = total[b * SLOT : (b + 1) * SLOT]
        product = g_nat[k] / (BINS * (TM // GROUP)) + RIDGE_WEIGHT * d32[k]
        new_residual = r32[k] - step_sizes[k] * product
        residual_out[:, k * COLS : (k + 1) * COLS] = new_residual
        nn_send[k : k + 1, :] = jnp.sum(new_residual * new_residual, axis=0, keepdims=True)

    def nn_copy(step):
        return remote(nn_send, nn_recv.at[step], nn_sem, step, tm_peer(step), z)

    each(1, TM, lambda step: nn_copy(step).start())
    each(1, TM, lambda step: nn_copy(step).wait_recv())
    nz_send[...] = nn_send[...] + jnp.sum(nn_recv[1:TM], axis=0)

    def nz_copy(step):
        return remote(nz_send, nz_recv.at[step], nz_sem, step, me, z_peer(step))

    each(1, NIN, lambda step: nz_copy(step).start())
    each(1, NIN, lambda step: nz_copy(step).wait_recv())
    new_norm = nz_send[...] + jnp.sum(nz_recv[1:NIN], axis=0)
    for k in range(GROUP):
        columns = slice(k * COLS, (k + 1) * COLS)
        ratio = new_norm[k : k + 1, :] / (old_norm[k : k + 1, :] + NORM_EPS)
        direction_out[:, columns] = residual_out[:, columns] + ratio * d32[k]

    each(1, GROUP, lambda step: spikes_copy(step).wait_send())

    @pl.when(sends_halo)
    def _():
        each(0, GROUP, lambda k: halo_copy(k).wait_send())

    each(1, GROUP, lambda step: tick_copy(step).wait_send())
    for copy in (direction_copy, nd_copy, gram_copy, c2_copy, nn_copy):
        each(1, TM, lambda step: copy(step).wait_send())
    for copy in (predictor_copy, cv_copy, nz_copy):
        each(1, NIN, lambda step: copy(step).wait_send())
    for half in range(2):
        each(1, NIN, lambda step: along_copy(half, step).wait_send())
        each(1, NIN, lambda step: weighted_arrival(half, step).wait_send())


def per_device(spikes, exposure, weights, direction, residual, iterate):
    table = lag_table()
    lag = jnp.asarray(table, BF16)
    lag_t = jnp.asarray(np.ascontiguousarray(table.T), BF16)
    rows, columns = direction.shape
    vmem = pl.BlockSpec(memory_space=pltpu.VMEM)
    hbm = pl.BlockSpec(memory_space=pl.ANY)
    pair = lambda n: pltpu.SemaphoreType.DMA((2, n))
    scratch = [
        pltpu.VMEM((OWN, NEUR), jnp.int32),
        pltpu.VMEM((BASES * HISTORY, 2 * HISTORY), BF16),
        pltpu.VMEM((2 * HISTORY, BASES * HISTORY), BF16),
        pltpu.VMEM((GROUP, rows, COLS), F32),
        pltpu.VMEM((GROUP, rows, COLS), F32),
        pltpu.VMEM((GROUP, rows, COLS), F32),
        pltpu.VMEM((FEAT, COLS), BF16),
        pltpu.VMEM((FEAT, COLS), F32),
        pltpu.VMEM((FEAT, COLS), BF16),
        pltpu.VMEM((HISTORY + BINS, NEUR), BF16),
        pltpu.VMEM((NEUR, HISTORY + BINS), BF16),
        pltpu.VMEM((BINS, FEAT), BF16),
        pltpu.VMEM((TM, BASES, SLOT, BINS), BF16),
        pltpu.VMEM((GROUP, BASES, SLOT, COLS), BF16),
        pltpu.VMEM((BASES, NEUR, COLS), BF16),
        pltpu.VMEM((2, NIN, 64, COLS), F32),
        pltpu.VMEM((2, NIN, 64, COLS), BF16),
        pltpu.VMEM((2, NIN, 64, COLS), BF16),
        pltpu.VMEM((2, NIN, 64, COLS), F32),
        pltpu.VMEM((2, NIN, 64, COLS), BF16),
        pltpu.VMEM((2, NIN, 64, COLS), BF16),
        pltpu.VMEM((2, NIN, 64, COLS), BF16),
        pltpu.VMEM((TM, rows, COLS), BF16),
        pltpu.VMEM((TM, rows, COLS), BF16),
        pltpu.VMEM((GROUP, rows, COLS), F32),
        pltpu.VMEM((GROUP, 8, COLS), F32),
        pltpu.VMEM((COLS, COLS), F32),
        pltpu.VMEM((8, COLS), F32),
        pltpu.VMEM((TM, 8, COLS), F32),
        pltpu.VMEM((16, COLS), F32),
        pltpu.VMEM((NIN, 16, COLS), F32),
        pltpu.VMEM((8, COLS), F32),
        pltpu.VMEM((TM, 8, COLS), F32),
        pltpu.VMEM((8, COLS), F32),
        pltpu.VMEM((TM, 8, COLS), F32),
        pltpu.VMEM((8, COLS), F32),
        pltpu.VMEM((NIN, 8, COLS), F32),
        pltpu.SemaphoreType.DMA((16,)),
        pair(GROUP), pair(GROUP), pair(GROUP),
        pair(TM), pair(NIN), pair(2 * NIN), pair(2 * NIN), pair(TM),
        pair(TM), pair(NIN), pair(TM), pair(TM), pair(NIN),
    ]
    return pl.pallas_call(
        kernel,
        out_shape=[jax.ShapeDtypeStruct((rows, columns), F32)] * 3,
        in_specs=[vmem] + [hbm] * 7,
        out_specs=[vmem] * 3,
        scratch_shapes=scratch,
        compiler_params=pltpu.CompilerParams(
            collective_id=0, has_side_effects=True, vmem_limit_bytes=40 * 2**20
        ),
    )(exposure.reshape(2, COLS), spikes, weights, direction, residual, iterate, lag, lag_t)


def solution(mesh):
    in_specs = (
        P("tm", "nin"),
        P("tm"),
        P("nin", "nout"),
        P(("nin", "tm"), "nout"),
        P(("nin", "tm"), "nout"),
        P(("nin", "tm"), "nout"),
    )
    out_specs = (P(("nin", "tm"), "nout"), P(("nin", "tm"), "nout"), P(("nin", "tm"), "nout"))
    return jax.shard_map(
        per_device, mesh=mesh, in_specs=in_specs, out_specs=out_specs, check_vma=False
    )
```

```python
import functools
import math

import jax
import jax.numpy as jnp
import numpy as np
from jax import lax
from jax.experimental import pallas as pl
from jax.experimental.pallas import tpu as pltpu
from jax.sharding import PartitionSpec as P

BASES = 8
HISTORY = 128
RIDGE_WEIGHT = 0.05
NORM_EPS = 1e-06
MESH = pl.DeviceIdType.MESH
F32 = jnp.float32
BF16 = jnp.bfloat16

TM = 16
NIN = 8
GROUP = 4
BINS = 1024
OWN = 256
NEUR = 256
COLS = 128
FEAT = NEUR * BASES
SLOT = NEUR // TM


def basis_table():
    lag_values = np.arange(1, HISTORY + 1, dtype=np.float32)
    warped = np.log(lag_values + np.float32(1.0))
    log_low = math.log(2.0)
    log_high = math.log(HISTORY + 1.0)
    spacing = (log_high - log_low) / (BASES - 1)
    centers = np.float32(log_low) + np.float32(spacing) * np.arange(BASES, dtype=np.float32)
    phases = (warped[:, None] - centers[None, :]) * np.float32(math.pi / (2.0 * spacing))
    phases = np.clip(phases, np.float32(-math.pi), np.float32(math.pi))
    bumps = np.float32(0.5) * (np.float32(1.0) + np.cos(phases))
    bumps = bumps / np.sum(bumps, axis=0, keepdims=True)
    return bumps.astype(np.float32)


def lag_table():
    basis = basis_table()
    lag = np.arange(HISTORY)[:, None] + HISTORY - np.arange(2 * HISTORY)[None, :]
    valid = (lag >= 1) & (lag <= HISTORY)
    table = np.where(valid[None], basis.T[:, np.clip(lag - 1, 0, HISTORY - 1)], np.float32(0.0))
    return table.reshape(BASES * HISTORY, 2 * HISTORY)


def kernel(
    exposure_ref, spikes_hbm, weights_hbm, direction_hbm, residual_hbm, lag_hbm, lag_t_hbm,
    product_out, step_out, ratio_out,
    spikes_in, lag, lag_t, d32, r32, w16, w32, wp, spk, spk_t, x, xt,
    d_send, d_all, p_own, p_send, p_recv, a_own, a_send, a_recv, wt_all, g_send, g_recv, g_nat,
    ticks, ticks_t, nd_send, nd_recv, cv_send, cv_recv, c2_send, c2_recv, nn_send, nn_recv, nz_send, nz_recv,
    load_sem, spk_sem, halo_sem, tick_sem, d_sem, p_sem, a_sem, wt_sem, g_sem, nd_sem, cv_sem, c2_sem, nn_sem, nz_sem,
):
    me = lax.axis_index("tm")
    z = lax.axis_index("nin")
    xo = lax.axis_index("nout")
    team = me // GROUP
    part = lax.rem(me, GROUP)

    def tm_peer(step):
        return lax.rem(me + step, TM)

    def z_peer(step):
        return lax.rem(z + step, NIN)

    def team_peer(step):
        return team * GROUP + lax.rem(part + step, GROUP)

    def remote(src, dst, sems, slot, tm_index, z_index):
        return pltpu.make_async_remote_copy(
            src_ref=src, dst_ref=dst, send_sem=sems.at[0, slot], recv_sem=sems.at[1, slot],
            device_id=(tm_index, z_index, xo), device_id_type=MESH,
        )

    def each(first, last, body):
        def run(step, carry):
            body(step)
            return carry

        lax.fori_loop(first, last, run, 0)

    loads = [
        pltpu.make_async_copy(spikes_hbm, spikes_in, load_sem.at[0]),
        pltpu.make_async_copy(lag_hbm, lag, load_sem.at[1]),
        pltpu.make_async_copy(lag_t_hbm, lag_t, load_sem.at[2]),
        pltpu.make_async_copy(
            weights_hbm.at[:, pl.ds(pl.multiple_of(part * COLS, COLS), COLS)], w16, load_sem.at[3]
        ),
    ]
    blocks = [
        [
            pltpu.make_async_copy(source.at[:, k * COLS : (k + 1) * COLS], target.at[k], load_sem.at[4 + 4 * n + k])
            for k in range(GROUP)
        ]
        for n, (source, target) in enumerate(((direction_hbm, d32), (residual_hbm, r32)))
    ]
    for copy in blocks[0] + loads[:1]:
        copy.start()
    for copy in loads[1:] + blocks[1]:
        copy.start()

    barrier = pltpu.get_barrier_semaphore()

    def greet_tm(step):
        pl.semaphore_signal(barrier, inc=1, device_id=(tm_peer(step), z, xo), device_id_type=MESH)

    def greet_z(step):
        pl.semaphore_signal(barrier, inc=1, device_id=(me, z_peer(step), xo), device_id_type=MESH)

    each(1, TM, greet_tm)
    each(1, NIN, greet_z)

    for copy in blocks[0]:
        copy.wait()
    for k in range(GROUP):
        for b in range(BASES):
            d_send[k, b] = d32[k, pl.ds(b, SLOT, stride=BASES), :].astype(BF16)
    loads[0].wait()
    own_rows = pl.ds(pl.multiple_of(HISTORY + part * OWN, HISTORY), OWN)
    spk[own_rows, :] = spikes_in[...].astype(F32).astype(BF16)
    ticks[part, 0:2, :] = exposure_ref[...].astype(F32) / 8.0
    ticks[part, 2:8, :] = jnp.zeros((6, COLS), F32)
    pl.semaphore_wait(barrier, TM - 1 + NIN - 1)

    def spikes_copy(step):
        return remote(spk.at[own_rows], spk.at[own_rows], spk_sem, step, team_peer(step), z)

    def spikes_arrival(step):
        rows = pl.ds(pl.multiple_of(HISTORY + lax.rem(part + GROUP - step, GROUP) * OWN, HISTORY), OWN)
        return remote(spk.at[rows], spk.at[rows], spk_sem, step, team_peer(step), z)

    def halo_copy(k):
        return remote(
            spk.at[BINS : BINS + HISTORY], spk.at[0:HISTORY], halo_sem, k, lax.rem((team + 1) * GROUP + k, TM), z
        )

    def tick_copy(step):
        return remote(ticks.at[part], ticks.at[part], tick_sem, step, team_peer(step), z)

    def tick_arrival(step):
        slot = lax.rem(part + GROUP - step, GROUP)
        return remote(ticks.at[slot], ticks.at[slot], tick_sem, step, team_peer(step), z)

    d_rows = pl.ds(pl.multiple_of(me * SLOT, SLOT), SLOT)

    def direction_copy(step):
        peer = tm_peer(step)
        return remote(d_send.at[lax.rem(peer, GROUP)], d_all.at[:, d_rows, :], d_sem, step, peer, z)

    def direction_arrival(step):
        rows = pl.ds(pl.multiple_of(tm_peer(TM - step) * SLOT, SLOT), SLOT)
        return remote(d_send.at[0], d_all.at[:, rows, :], d_sem, step, tm_peer(step), z)

    sends_halo = jnp.logical_and(part == GROUP - 1, team < TM // GROUP - 1)

    each(1, GROUP, lambda step: spikes_copy(step).start())

    @pl.when(sends_halo)
    def _():
        each(0, GROUP, lambda k: halo_copy(k).start())

    each(1, TM, lambda step: direction_copy(step).start())
    each(1, GROUP, lambda step: tick_copy(step).start())
    d_all[:, d_rows, :] = d_send[part]

    for copy in blocks[1]:
        copy.wait()
    for k in range(GROUP):
        nd_send[k : k + 1, :] = jnp.sum(r32[k] * r32[k], axis=0, keepdims=True)
        nd_send[GROUP + k : GROUP + k + 1, :] = jnp.sum(d32[k] * d32[k], axis=0, keepdims=True)

    def nd_copy(step):
        return remote(nd_send, nd_recv.at[step], nd_sem, step, tm_peer(step), z)

    each(1, TM, lambda step: nd_copy(step).start())

    loads[3].wait()
    w32[...] = w16[...].astype(F32)
    for b in range(BASES):
        wp[b * NEUR : (b + 1) * NEUR, :] = w32[pl.ds(b, NEUR, stride=BASES), :].astype(BF16)
    loads[1].wait()
    loads[2].wait()

    @pl.when(team == 0)
    def _():
        spk[0:HISTORY, :] = jnp.zeros((HISTORY, NEUR), BF16)

    @pl.when(team > 0)
    def _():
        pltpu.make_async_remote_copy(
            src_ref=spk.at[0:HISTORY], dst_ref=spk.at[0:HISTORY], send_sem=halo_sem.at[0, part],
            recv_sem=halo_sem.at[1, part], device_id=(me, z, xo), device_id_type=MESH,
        ).wait_recv()

    each(1, GROUP, lambda step: spikes_arrival(step).wait_recv())

    for n in range(9):
        spk_t[:, n * HISTORY : (n + 1) * HISTORY] = spk[n * HISTORY : (n + 1) * HISTORY, :].astype(F32).T.astype(BF16)

    def features(block):
        rows = pl.ds(pl.multiple_of(block * HISTORY, HISTORY), HISTORY)
        window = pl.ds(pl.multiple_of(block * HISTORY, HISTORY), 2 * HISTORY)
        made = jnp.dot(lag[...], spk[window, :], preferred_element_type=F32)
        for b in range(BASES):
            x[rows, b * NEUR : (b + 1) * NEUR] = made[b * HISTORY : (b + 1) * HISTORY].astype(BF16)
        made_t = jnp.dot(spk_t[:, window], lag_t[...], preferred_element_type=F32)
        for b in range(BASES):
            piece = made_t[:, b * HISTORY : (b + 1) * HISTORY].astype(BF16)
            xt[:, b, :, rows] = piece.reshape(TM, SLOT, HISTORY)

    each(0, BINS // HISTORY, features)

    def predictor(half):
        rows = pl.ds(pl.multiple_of(half * 512, 512), 512)
        made = jnp.dot(x[rows, :], wp[...], preferred_element_type=F32).reshape(NIN, 64, COLS)
        p_own[half] = made
        p_send[half] = made.astype(BF16)

    each(0, 2, predictor)

    def predictor_copy(step):
        return remote(p_send.at[:, z_peer(step)], p_recv.at[:, step], p_sem, step, me, z_peer(step))

    each(1, NIN, lambda step: predictor_copy(step).start())

    each(1, TM, lambda step: direction_arrival(step).wait_recv())

    def along_copy(half, step):
        return remote(a_send.at[half, z_peer(step)], a_recv.at[half, step], a_sem, half * NIN + step, me, z_peer(step))

    def along(half):
        rows = pl.ds(pl.multiple_of(half * 512, 512), 512)
        made = jnp.dot(x[rows, :], d_all[...].reshape(FEAT, COLS), preferred_element_type=F32).reshape(NIN, 64, COLS)
        a_own[half] = made
        a_send[half] = made.astype(BF16)
        each(1, NIN, lambda step: along_copy(half, step).start())

    each(0, 2, along)

    each(1, GROUP, lambda step: tick_arrival(step).wait_recv())
    table = jnp.concatenate([ticks[k, 0:2, :] for k in range(GROUP)] + [jnp.zeros((COLS - 8, COLS), F32)], axis=0)
    ticks_t[...] = table.T
    tick_rows = ticks_t[pl.ds(pl.multiple_of(lax.rem(z, 2) * 64, 64), 64), :]
    lane = lax.broadcasted_iota(jnp.int32, (64, COLS), 1)

    each(1, TM, lambda step: nd_copy(step).wait_recv())
    cv_send[0:8, :] = nd_send[...] + jnp.sum(nd_recv[1:TM], axis=0)

    each(1, NIN, lambda step: predictor_copy(step).wait_recv())
    curvature_part = jnp.zeros((1, COLS), F32)
    for half in range(2):
        each(1, NIN, lambda step: along_copy(half, step).wait_recv())
        p_sum = p_own[half, z]
        a_sum = a_own[half, z]
        for step in range(1, NIN):
            p_sum += p_recv[half, step].astype(F32)
            a_sum += a_recv[half, step].astype(F32)
        scale = jnp.sum(jnp.where(lane == half * 4 + z // 2, tick_rows, 0.0), axis=1, keepdims=True)
        weighted = ((scale * jnp.exp(p_sum)) * a_sum).astype(BF16)
        wt_all[half, z] = weighted
        each(
            1, NIN,
            lambda step: remote(
                wt_all.at[half, z], wt_all.at[half, z], wt_sem, half * NIN + step, me, z_peer(step)
            ).start(),
        )
        curvature_part += jnp.sum(weighted.astype(F32) * a_sum, axis=0, keepdims=True)
    cv_send[8:16, :] = jnp.concatenate([curvature_part, jnp.zeros((7, COLS), F32)], axis=0)

    def cv_copy(step):
        return remote(cv_send, cv_recv.at[step], cv_sem, step, me, z_peer(step))

    each(1, NIN, lambda step: cv_copy(step).start())

    def weighted_arrival(half, step):
        slot = z_peer(NIN - step)
        return remote(wt_all.at[half, slot], wt_all.at[half, slot], wt_sem, half * NIN + step, me, z_peer(step))

    for half in range(2):
        each(1, NIN, lambda step: weighted_arrival(half, step).wait_recv())

    def gram_copy(step):
        return remote(g_send.at[tm_peer(step)], g_recv.at[me], g_sem, step, tm_peer(step), z)

    def gram_to(peer):
        return remote(g_send.at[peer], g_recv.at[me], g_sem, lax.rem(peer + TM - me, TM), peer, z)

    def gram_arrival(step):
        return remote(g_send.at[0], g_recv.at[tm_peer(TM - step)], g_sem, step, tm_peer(step), z)

    def gram(turn):
        group = lax.rem(team + turn, GROUP)
        rows = pl.ds(group * 4, 4)
        made = jnp.dot(
            xt[rows].reshape(4 * SLOT * BASES, BINS), wt_all[...].reshape(BINS, COLS), preferred_element_type=F32
        )
        g_send[rows] = made.astype(BF16).reshape(4, SLOT * BASES, COLS)

        @pl.when(turn < 4)
        def _():
            each(0, GROUP, lambda k: gram_to(group * GROUP + k).start())

    each(1, 5, gram)
    each(1, GROUP, lambda step: gram_to(team_peer(step)).start())
    g_recv[me] = g_send[me]

    each(1, NIN, lambda step: cv_copy(step).wait_recv())
    cv_sum = cv_send[...] + jnp.sum(cv_recv[1:NIN], axis=0)
    old_norm = cv_sum[0:4, :]
    c2_send[...] = cv_sum[8:16, :]
    c2_recv[me] = cv_sum[8:16, :]

    def c2_copy(step):
        return remote(c2_send, c2_recv.at[me], c2_sem, step, tm_peer(step), z)

    def c2_arrival(step):
        return remote(c2_send, c2_recv.at[tm_peer(TM - step)], c2_sem, step, tm_peer(step), z)

    each(1, TM, lambda step: c2_copy(step).start())
    each(1, TM, lambda step: c2_arrival(step).wait_recv())
    step_sizes = []
    for k in range(GROUP):
        total = c2_recv[k, 0:1, :]
        for t in range(1, TM // GROUP):
            total += c2_recv[t * GROUP + k, 0:1, :]
        curvature = total / (BINS * (TM // GROUP)) + RIDGE_WEIGHT * cv_sum[4 + k : 5 + k, :]
        step_size = old_norm[k : k + 1, :] / curvature
        step_sizes.append(step_size)
        step_out[:, k * COLS : (k + 1) * COLS] = step_size

    each(1, TM, lambda step: gram_arrival(step).wait_recv())
    nn_send[4:8, :] = jnp.zeros((4, COLS), F32)
    for k in range(GROUP):
        total = g_recv[k].astype(F32)
        for t in range(1, TM // GROUP):
            total += g_recv[t * GROUP + k].astype(F32)
        for b in range(BASES):
            g_nat[k, pl.ds(b, SLOT, stride=BASES), :] = total[b * SLOT : (b + 1) * SLOT]
        product = g_nat[k] / (BINS * (TM // GROUP)) + RIDGE_WEIGHT * d32[k]
        new_residual = r32[k] - step_sizes[k] * product
        product_out[:, k * COLS : (k + 1) * COLS] = product
        nn_send[k : k + 1, :] = jnp.sum(new_residual * new_residual, axis=0, keepdims=True)

    def nn_copy(step):
        return remote(nn_send, nn_recv.at[step], nn_sem, step, tm_peer(step), z)

    each(1, TM, lambda step: nn_copy(step).start())
    each(1, TM, lambda step: nn_copy(step).wait_recv())
    nz_send[...] = nn_send[...] + jnp.sum(nn_recv[1:TM], axis=0)

    def nz_copy(step):
        return remote(nz_send, nz_recv.at[step], nz_sem, step, me, z_peer(step))

    each(1, NIN, lambda step: nz_copy(step).start())
    each(1, NIN, lambda step: nz_copy(step).wait_recv())
    new_norm = nz_send[...] + jnp.sum(nz_recv[1:NIN], axis=0)
    for k in range(GROUP):
        ratio = new_norm[k : k + 1, :] / (old_norm[k : k + 1, :] + NORM_EPS)
        ratio_out[:, k * COLS : (k + 1) * COLS] = ratio

    each(1, GROUP, lambda step: spikes_copy(step).wait_send())

    @pl.when(sends_halo)
    def _():
        each(0, GROUP, lambda k: halo_copy(k).wait_send())

    each(1, GROUP, lambda step: tick_copy(step).wait_send())
    for copy in (direction_copy, nd_copy, gram_copy, c2_copy, nn_copy):
        each(1, TM, lambda step: copy(step).wait_send())
    for copy in (predictor_copy, cv_copy, nz_copy):
        each(1, NIN, lambda step: copy(step).wait_send())
    for half in range(2):
        each(1, NIN, lambda step: along_copy(half, step).wait_send())
        each(1, NIN, lambda step: weighted_arrival(half, step).wait_send())


def per_device(spikes, exposure, weights, direction, residual, iterate):
    table = lag_table()
    lag = jnp.asarray(table, BF16)
    lag_t = jnp.asarray(np.ascontiguousarray(table.T), BF16)
    rows, columns = direction.shape
    vmem = pl.BlockSpec(memory_space=pltpu.VMEM)
    hbm = pl.BlockSpec(memory_space=pl.ANY)
    pair = lambda n: pltpu.SemaphoreType.DMA((2, n))
    scratch = [
        pltpu.VMEM((OWN, NEUR), jnp.int32),
        pltpu.VMEM((BASES * HISTORY, 2 * HISTORY), BF16),
        pltpu.VMEM((2 * HISTORY, BASES * HISTORY), BF16),
        pltpu.VMEM((GROUP, rows, COLS), F32),
        pltpu.VMEM((GROUP, rows, COLS), F32),
        pltpu.VMEM((FEAT, COLS), BF16),
        pltpu.VMEM((FEAT, COLS), F32),
        pltpu.VMEM((FEAT, COLS), BF16),
        pltpu.VMEM((HISTORY + BINS, NEUR), BF16),
        pltpu.VMEM((NEUR, HISTORY + BINS), BF16),
        pltpu.VMEM((BINS, FEAT), BF16),
        pltpu.VMEM((TM, BASES, SLOT, BINS), BF16),
        pltpu.VMEM((GROUP, BASES, SLOT, COLS), BF16),
        pltpu.VMEM((BASES, NEUR, COLS), BF16),
        pltpu.VMEM((2, NIN, 64, COLS), F32),
        pltpu.VMEM((2, NIN, 64, COLS), BF16),
        pltpu.VMEM((2, NIN, 64, COLS), BF16),
        pltpu.VMEM((2, NIN, 64, COLS), F32),
        pltpu.VMEM((2, NIN, 64, COLS), BF16),
        pltpu.VMEM((2, NIN, 64, COLS), BF16),
        pltpu.VMEM((2, NIN, 64, COLS), BF16),
        pltpu.VMEM((TM, rows, COLS), BF16),
        pltpu.VMEM((TM, rows, COLS), BF16),
        pltpu.VMEM((GROUP, rows, COLS), F32),
        pltpu.VMEM((GROUP, 8, COLS), F32),
        pltpu.VMEM((COLS, COLS), F32),
        pltpu.VMEM((8, COLS), F32),
        pltpu.VMEM((TM, 8, COLS), F32),
        pltpu.VMEM((16, COLS), F32),
        pltpu.VMEM((NIN, 16, COLS), F32),
        pltpu.VMEM((8, COLS), F32),
        pltpu.VMEM((TM, 8, COLS), F32),
        pltpu.VMEM((8, COLS), F32),
        pltpu.VMEM((TM, 8, COLS), F32),
        pltpu.VMEM((8, COLS), F32),
        pltpu.VMEM((NIN, 8, COLS), F32),
        pltpu.SemaphoreType.DMA((16,)),
        pair(GROUP), pair(GROUP), pair(GROUP),
        pair(TM), pair(NIN), pair(2 * NIN), pair(2 * NIN), pair(TM),
        pair(TM), pair(NIN), pair(TM), pair(TM), pair(NIN),
    ]
    product, step_size, ratio = pl.pallas_call(
        kernel,
        out_shape=[jax.ShapeDtypeStruct((rows, columns), F32), *[jax.ShapeDtypeStruct((1, columns), F32)] * 2],
        in_specs=[vmem] + [hbm] * 6,
        out_specs=[vmem] * 3,
        scratch_shapes=scratch,
        compiler_params=pltpu.CompilerParams(
            collective_id=0, has_side_effects=True, vmem_limit_bytes=60 * 2**20
        ),
    )(exposure.reshape(2, COLS), spikes, weights, direction, residual, lag, lag_t)
    new_residual = residual - step_size * product
    return iterate + step_size * direction, new_residual, new_residual + ratio * direction


def solution(mesh):
    in_specs = (
        P("tm", "nin"),
        P("tm"),
        P("nin", "nout"),
        P(("nin", "tm"), "nout"),
        P(("nin", "tm"), "nout"),
        P(("nin", "tm"), "nout"),
    )
    out_specs = (P(("nin", "tm"), "nout"), P(("nin", "tm"), "nout"), P(("nin", "tm"), "nout"))
    return jax.shard_map(
        per_device, mesh=mesh, in_specs=in_specs, out_specs=out_specs, check_vma=False
    )
```

```python
import functools
import math

import jax
import jax.numpy as jnp
import numpy as np
from jax import lax
from jax.experimental import pallas as pl
from jax.experimental.pallas import tpu as pltpu
from jax.sharding import PartitionSpec as P

BASES = 8
HISTORY = 128
RIDGE_WEIGHT = 0.05
NORM_EPS = 1e-06
MESH = pl.DeviceIdType.MESH
F32 = jnp.float32
BF16 = jnp.bfloat16

TM = 16
NIN = 8
NOUT = 4
EARLY = 3
GROUP = 4
BINS = 1024
OWN = 256
NEUR = 256
COLS = 128
FEAT = NEUR * BASES
SLOT = NEUR // TM


def basis_table():
    lag_values = np.arange(1, HISTORY + 1, dtype=np.float32)
    warped = np.log(lag_values + np.float32(1.0))
    log_low = math.log(2.0)
    log_high = math.log(HISTORY + 1.0)
    spacing = (log_high - log_low) / (BASES - 1)
    centers = np.float32(log_low) + np.float32(spacing) * np.arange(BASES, dtype=np.float32)
    phases = (warped[:, None] - centers[None, :]) * np.float32(math.pi / (2.0 * spacing))
    phases = np.clip(phases, np.float32(-math.pi), np.float32(math.pi))
    bumps = np.float32(0.5) * (np.float32(1.0) + np.cos(phases))
    bumps = bumps / np.sum(bumps, axis=0, keepdims=True)
    return bumps.astype(np.float32)


def lag_table():
    basis = basis_table()
    lag = np.arange(HISTORY)[:, None] + HISTORY - np.arange(2 * HISTORY)[None, :]
    valid = (lag >= 1) & (lag <= HISTORY)
    table = np.where(valid[None], basis.T[:, np.clip(lag - 1, 0, HISTORY - 1)], np.float32(0.0))
    return table.reshape(BASES * HISTORY, 2 * HISTORY)


def kernel(
    exposure_ref, spikes_hbm, weights_hbm, direction_hbm, residual_hbm, lag_hbm, lag_t_hbm,
    product_out, step_out, ratio_out,
    spikes_in, lag, lag_t, d32, r32, w16, w32, wp, spk, spk_t, x, xt,
    d_send, d_all, p_own, p_send, p_recv, a_own, a_send, a_recv, wt_all, g_send, g_recv, g_nat,
    ticks, ticks_t, nd_send, nd_recv, cv_send, cv_recv, c2_send, c2_recv, nn_send, nn_recv, nz_send, nz_recv,
    load_sem, spk_sem, halo_sem, tick_sem, d_sem, p_sem, a_sem, wt_sem, g_sem, nd_sem, cv_sem, c2_sem, nn_sem, nz_sem,
):
    me = lax.axis_index("tm")
    z = lax.axis_index("nin")
    xo = lax.axis_index("nout")
    team = me // GROUP
    part = lax.rem(me, GROUP)

    def tm_peer(step):
        return lax.rem(me + step, TM)

    def z_peer(step):
        return lax.rem(z + step, NIN)

    def team_peer(step):
        return team * GROUP + lax.rem(part + step, GROUP)

    chip = me // 2
    core = lax.rem(me, 2)
    half_own = lax.rem(chip, 2)
    mate = chip + 1 - 2 * half_own

    def x_peer(step):
        return lax.rem(xo + step, NOUT)

    def swing(turn, middle):
        return middle + (1 - 2 * lax.rem(turn, 2)) * ((turn + 1) // 2)

    def remote(src, dst, sems, slot, tm_index, z_index, x_index=None):
        return pltpu.make_async_remote_copy(
            src_ref=src, dst_ref=dst, send_sem=sems.at[0, slot], recv_sem=sems.at[1, slot],
            device_id=(tm_index, z_index, xo if x_index is None else x_index), device_id_type=MESH,
        )

    def far_first(count, body):
        each(0, count - 1, lambda turn: body(swing(turn, count // 2)))

    def each(first, last, body):
        def run(step, carry):
            body(step)
            return carry

        lax.fori_loop(first, last, run, 0)

    loads = [
        pltpu.make_async_copy(spikes_hbm, spikes_in, load_sem.at[0]),
        pltpu.make_async_copy(lag_hbm, lag, load_sem.at[1]),
        pltpu.make_async_copy(lag_t_hbm, lag_t, load_sem.at[2]),
        pltpu.make_async_copy(
            weights_hbm.at[:, pl.ds(pl.multiple_of(part * COLS, COLS), COLS)], w16, load_sem.at[3]
        ),
    ]
    blocks = [
        [
            pltpu.make_async_copy(source.at[:, k * COLS : (k + 1) * COLS], target.at[k], load_sem.at[4 + 4 * n + k])
            for k in range(GROUP)
        ]
        for n, (source, target) in enumerate(((direction_hbm, d32), (residual_hbm, r32)))
    ]
    for copy in blocks[0] + loads[:1]:
        copy.start()
    for copy in loads[1:] + blocks[1]:
        copy.start()

    barrier = pltpu.get_barrier_semaphore()

    def greet_tm(step):
        pl.semaphore_signal(barrier, inc=1, device_id=(tm_peer(step), z, xo), device_id_type=MESH)

    def greet_z(step):
        pl.semaphore_signal(barrier, inc=1, device_id=(me, z_peer(step), xo), device_id_type=MESH)

    each(1, TM, greet_tm)
    each(1, NIN, greet_z)

    def greet_x(step):
        for c in range(2):
            pl.semaphore_signal(
                barrier, inc=1, device_id=(chip * 2 + c, z, x_peer(step)), device_id_type=MESH
            )

    each(1, NOUT, greet_x)

    for copy in blocks[0]:
        copy.wait()
    for k in range(GROUP):
        for b in range(BASES):
            d_send[k, b] = d32[k, pl.ds(b, SLOT, stride=BASES), :].astype(BF16)
    loads[0].wait()
    own_rows = pl.ds(pl.multiple_of(HISTORY + part * OWN, HISTORY), OWN)
    spk[own_rows, :] = spikes_in[...].astype(F32).astype(BF16)
    ticks[part, 0:2, :] = exposure_ref[...].astype(F32) / 8.0
    ticks[part, 2:8, :] = jnp.zeros((6, COLS), F32)
    pl.semaphore_wait(barrier, TM - 1 + NIN - 1 + 2 * (NOUT - 1))

    def core_copy():
        return remote(spk.at[own_rows], spk.at[own_rows], spk_sem, 8, chip * 2 + 1 - core, z)

    def core_arrival():
        rows = pl.ds(pl.multiple_of(HISTORY + (half_own * 2 + 1 - core) * OWN, HISTORY), OWN)
        return remote(spk.at[rows], spk.at[rows], spk_sem, 8, chip * 2 + 1 - core, z)

    def quarter(half, from_core, x_index):
        return pl.ds(pl.multiple_of(HISTORY + (half * 2 + from_core) * OWN + x_index * 64, 64), 64)

    def mate_copy():
        rows = quarter(half_own, core, xo)
        return remote(spk.at[rows], spk.at[rows], spk_sem, 0, mate * 2 + core, z)

    def mate_arrival(step, other):
        from_core = core if other == 0 else 1 - core
        rows = quarter(1 - half_own, from_core, x_peer(NOUT - step))
        return remote(spk.at[rows], spk.at[rows], spk_sem, step * 2 + other, me, z)

    def spread_copy(step, other):
        rows = quarter(1 - half_own, core, xo)
        to_core = core if other == 0 else 1 - core
        return remote(spk.at[rows], spk.at[rows], spk_sem, step * 2 + other, chip * 2 + to_core, z, x_peer(step))

    def halo_copy(k):
        rows = pl.ds(pl.multiple_of(BINS + xo * 32, 32), 32)
        return remote(
            spk.at[rows], spk.at[halo_rows(xo)], halo_sem, 8 + k, lax.rem((team + 1) * GROUP + 2 * k + 1, TM), z
        )

    def halo_rows(x_index):
        return pl.ds(pl.multiple_of(x_index * 32, 32), 32)

    def halo_first():
        rows = halo_rows(xo)
        return remote(spk.at[rows], spk.at[rows], halo_sem, 8 + half_own, me, z)

    def halo_spread(step, other):
        rows = halo_rows(xo)
        return remote(spk.at[rows], spk.at[rows], halo_sem, step * 2 + other, chip * 2 + 1 - other, z, x_peer(step))

    def halo_arrival(step):
        rows = halo_rows(x_peer(NOUT - step))
        return remote(spk.at[rows], spk.at[rows], halo_sem, step * 2 + 1 - core, me, z)

    def tick_copy(step):
        return remote(ticks.at[part], ticks.at[part], tick_sem, step, team_peer(step), z)

    def tick_arrival(step):
        slot = lax.rem(part + GROUP - step, GROUP)
        return remote(ticks.at[slot], ticks.at[slot], tick_sem, step, team_peer(step), z)

    d_rows = pl.ds(pl.multiple_of(me * SLOT, SLOT), SLOT)

    def direction_copy(step):
        peer = tm_peer(step)
        return remote(d_send.at[lax.rem(peer, GROUP)], d_all.at[:, d_rows, :], d_sem, step, peer, z)

    def direction_arrival(step):
        rows = pl.ds(pl.multiple_of(tm_peer(TM - step) * SLOT, SLOT), SLOT)
        return remote(d_send.at[0], d_all.at[:, rows, :], d_sem, step, tm_peer(step), z)

    sends_halo = jnp.logical_and(part == GROUP - 1, team < TM // GROUP - 1)
    hands_halo = jnp.logical_and(core == 1, team > 0)
    spreads = [(step, other) for step in (2, 1, 3, 0) for other in range(2) if (step, other) != (0, 0)]

    mate_copy().start()

    @pl.when(sends_halo)
    def _():
        halo_copy(0).start()
        halo_copy(1).start()

    core_copy().start()
    far_first(TM, lambda step: direction_copy(step).start())
    each(1, GROUP, lambda step: tick_copy(step).start())
    d_all[:, d_rows, :] = d_send[part]

    loads[3].wait()
    w32[...] = w16[...].astype(F32)
    for b in range(BASES):
        wp[b * NEUR : (b + 1) * NEUR, :] = w32[pl.ds(b, NEUR, stride=BASES), :].astype(BF16)

    def turn_spikes(n):
        rows = pl.ds(pl.multiple_of(n * HISTORY, HISTORY), HISTORY)
        spk_t[:, rows] = spk[rows, :].astype(F32).T.astype(BF16)

    own_first = half_own * 4 + 1

    def features(k):
        block = lax.rem(own_first + k, 8)
        rows = pl.ds(pl.multiple_of(k * HISTORY, HISTORY), HISTORY)
        window = pl.ds(pl.multiple_of(block * HISTORY, HISTORY), 2 * HISTORY)
        made = jnp.dot(lag[...], spk[window, :], preferred_element_type=F32)
        for b in range(BASES):
            x[rows, b * NEUR : (b + 1) * NEUR] = made[b * HISTORY : (b + 1) * HISTORY].astype(BF16)
        made_t = jnp.dot(spk_t[:, window], lag_t[...], preferred_element_type=F32)
        for b in range(BASES):
            piece = made_t[:, b * HISTORY : (b + 1) * HISTORY].astype(BF16)
            xt[:, b, :, rows] = piece.reshape(TM, SLOT, HISTORY)

    loads[1].wait()
    loads[2].wait()
    core_arrival().wait_recv()
    each(0, 4, lambda k: turn_spikes(own_first + k))
    each(0, EARLY, features)

    mate_arrival(0, 0).wait_recv()
    for step, other in spreads:
        spread_copy(step, other).start()

    @pl.when(team == 0)
    def _():
        spk[0:HISTORY, :] = jnp.zeros((HISTORY, NEUR), BF16)

    @pl.when(hands_halo)
    def _():
        halo_first().wait_recv()
        for step, other in spreads:
            halo_spread(step, other).start()

    def predictor(first, last):
        made = jnp.dot(x[first * HISTORY : last * HISTORY, :], wp[...], preferred_element_type=F32)
        made = made.reshape(last - first, NIN, 16, COLS)
        p_own[first:last] = made
        p_send[first:last] = made.astype(BF16)

    def predictor_copy(late, step):
        blocks_of = slice(EARLY, 8) if late else slice(0, EARLY)
        return remote(
            p_send.at[blocks_of, z_peer(step)], p_recv.at[blocks_of, step], p_sem, late * NIN + step, me, z_peer(step)
        )

    predictor(0, EARLY)
    far_first(NIN, lambda step: predictor_copy(0, step).start())

    for copy in blocks[1]:
        copy.wait()
    for k in range(GROUP):
        nd_send[k : k + 1, :] = jnp.sum(r32[k] * r32[k], axis=0, keepdims=True)
        nd_send[GROUP + k : GROUP + k + 1, :] = jnp.sum(d32[k] * d32[k], axis=0, keepdims=True)

    def nd_copy(step):
        return remote(nd_send, nd_recv.at[step], nd_sem, step, tm_peer(step), z)

    each(1, TM, lambda step: nd_copy(step).start())

    for step, other in spreads:
        mate_arrival(step, other).wait_recv()

    @pl.when(team > 0)
    def _():
        each(core, NOUT, lambda step: halo_arrival(step).wait_recv())

    each(0, 5, lambda k: turn_spikes(lax.rem(own_first + 4 + k, 9)))
    each(EARLY, 8, features)
    predictor(EARLY, 8)
    far_first(NIN, lambda step: predictor_copy(1, step).start())

    each(1, TM, lambda step: direction_arrival(step).wait_recv())

    def along_copy(half, step):
        blocks_of = slice(half * 4, half * 4 + 4)
        return remote(
            a_send.at[blocks_of, z_peer(step)], a_recv.at[blocks_of, step], a_sem, half * NIN + step, me, z_peer(step)
        )

    for half in range(2):
        made = jnp.dot(
            x[half * 512 : half * 512 + 512, :], d_all[...].reshape(FEAT, COLS), preferred_element_type=F32
        ).reshape(4, NIN, 16, COLS)
        a_own[half * 4 : half * 4 + 4] = made
        a_send[half * 4 : half * 4 + 4] = made.astype(BF16)
        far_first(NIN, lambda step: along_copy(half, step).start())

    each(1, GROUP, lambda step: tick_arrival(step).wait_recv())
    table = jnp.concatenate([ticks[k, 0:2, :] for k in range(GROUP)] + [jnp.zeros((COLS - 8, COLS), F32)], axis=0)
    ticks_t[...] = table.T
    tick_rows = ticks_t[pl.ds(pl.multiple_of(z * 16, 16), 16), :]
    lane = lax.broadcasted_iota(jnp.int32, (16, COLS), 1)

    each(1, TM, lambda step: nd_copy(step).wait_recv())
    cv_send[0:8, :] = nd_send[...] + jnp.sum(nd_recv[1:TM], axis=0)

    for late in range(2):
        each(1, NIN, lambda step: predictor_copy(late, step).wait_recv())

    def weighted_copy(half, slot, step):
        place = wt_all.at[slice(half * 4, half * 4 + 4), slot]
        return remote(place, place, wt_sem, half * NIN + step, me, z_peer(step))

    curvature_part = jnp.zeros((1, COLS), F32)
    for half in range(2):
        each(1, NIN, lambda step: along_copy(half, step).wait_recv())
        for k in range(half * 4, half * 4 + 4):
            p_sum = p_own[k, z]
            a_sum = a_own[k, z]
            for step in range(1, NIN):
                p_sum += p_recv[k, step].astype(F32)
                a_sum += a_recv[k, step].astype(F32)
            scale = jnp.sum(jnp.where(lane == lax.rem(own_first + k, 8), tick_rows, 0.0), axis=1, keepdims=True)
            weighted = ((scale * jnp.exp(p_sum)) * a_sum).astype(BF16)
            wt_all[k, z] = weighted
            curvature_part += jnp.sum(weighted.astype(F32) * a_sum, axis=0, keepdims=True)
        far_first(NIN, lambda step: weighted_copy(half, z, step).start())
    cv_send[8:16, :] = jnp.concatenate([curvature_part, jnp.zeros((7, COLS), F32)], axis=0)

    def cv_copy(step):
        return remote(cv_send, cv_recv.at[step], cv_sem, step, me, z_peer(step))

    each(1, NIN, lambda step: cv_copy(step).start())

    for half in range(2):
        each(1, NIN, lambda step: weighted_copy(half, z_peer(NIN - step), step).wait_recv())

    def gram_copy(step):
        return remote(g_send.at[tm_peer(step)], g_recv.at[me], g_sem, step, tm_peer(step), z)

    def gram_to(peer):
        return remote(g_send.at[peer], g_recv.at[me], g_sem, lax.rem(peer + TM - me, TM), peer, z)

    def gram_arrival(step):
        return remote(g_send.at[0], g_recv.at[tm_peer(TM - step)], g_sem, step, tm_peer(step), z)

    def gram(turn):
        group = lax.rem(team + swing(turn, 2), GROUP)
        rows = pl.ds(group * 4, 4)
        made = jnp.dot(
            xt[rows].reshape(4 * SLOT * BASES, BINS), wt_all[...].reshape(BINS, COLS), preferred_element_type=F32
        )
        g_send[rows] = made.astype(BF16).reshape(4, SLOT * BASES, COLS)

        @pl.when(turn < 3)
        def _():
            each(0, GROUP, lambda k: gram_to(group * GROUP + k).start())

    each(0, 4, gram)
    each(1, GROUP, lambda step: gram_to(team_peer(step)).start())
    g_recv[me] = g_send[me]

    each(1, NIN, lambda step: cv_copy(step).wait_recv())
    cv_sum = cv_send[...] + jnp.sum(cv_recv[1:NIN], axis=0)
    old_norm = cv_sum[0:4, :]
    c2_send[...] = cv_sum[8:16, :]
    c2_recv[me] = cv_sum[8:16, :]

    def c2_copy(step):
        return remote(c2_send, c2_recv.at[me], c2_sem, step, tm_peer(step), z)

    def c2_arrival(step):
        return remote(c2_send, c2_recv.at[tm_peer(TM - step)], c2_sem, step, tm_peer(step), z)

    each(1, TM, lambda step: c2_copy(step).start())
    each(1, TM, lambda step: c2_arrival(step).wait_recv())
    step_sizes = []
    for k in range(GROUP):
        total = c2_recv[k, 0:1, :]
        for t in range(1, TM // GROUP):
            total += c2_recv[t * GROUP + k, 0:1, :]
        curvature = total / (BINS * (TM // GROUP)) + RIDGE_WEIGHT * cv_sum[4 + k : 5 + k, :]
        step_size = old_norm[k : k + 1, :] / curvature
        step_sizes.append(step_size)
        step_out[:, k * COLS : (k + 1) * COLS] = step_size

    each(1, TM, lambda step: gram_arrival(step).wait_recv())
    nn_send[4:8, :] = jnp.zeros((4, COLS), F32)
    for k in range(GROUP):
        total = g_recv[k].astype(F32)
        for t in range(1, TM // GROUP):
            total += g_recv[t * GROUP + k].astype(F32)
        for b in range(BASES):
            g_nat[k, pl.ds(b, SLOT, stride=BASES), :] = total[b * SLOT : (b + 1) * SLOT]
        product = g_nat[k] / (BINS * (TM // GROUP)) + RIDGE_WEIGHT * d32[k]
        new_residual = r32[k] - step_sizes[k] * product
        product_out[:, k * COLS : (k + 1) * COLS] = product
        nn_send[k : k + 1, :] = jnp.sum(new_residual * new_residual, axis=0, keepdims=True)

    def nn_copy(step):
        return remote(nn_send, nn_recv.at[step], nn_sem, step, tm_peer(step), z)

    far_first(TM, lambda step: nn_copy(step).start())
    each(1, TM, lambda step: nn_copy(step).wait_recv())
    nz_send[...] = nn_send[...] + jnp.sum(nn_recv[1:TM], axis=0)

    def nz_copy(step):
        return remote(nz_send, nz_recv.at[step], nz_sem, step, me, z_peer(step))

    far_first(NIN, lambda step: nz_copy(step).start())
    each(1, NIN, lambda step: nz_copy(step).wait_recv())
    new_norm = nz_send[...] + jnp.sum(nz_recv[1:NIN], axis=0)
    for k in range(GROUP):
        ratio = new_norm[k : k + 1, :] / (old_norm[k : k + 1, :] + NORM_EPS)
        ratio_out[:, k * COLS : (k + 1) * COLS] = ratio

    mate_copy().wait_send()
    core_copy().wait_send()
    for step, other in spreads:
        spread_copy(step, other).wait_send()

    @pl.when(sends_halo)
    def _():
        halo_copy(0).wait_send()
        halo_copy(1).wait_send()

    @pl.when(hands_halo)
    def _():
        for step, other in spreads:
            halo_spread(step, other).wait_send()

    each(1, GROUP, lambda step: tick_copy(step).wait_send())
    for copy in (direction_copy, nd_copy, gram_copy, c2_copy, nn_copy):
        each(1, TM, lambda step: copy(step).wait_send())
    for copy in (cv_copy, nz_copy):
        each(1, NIN, lambda step: copy(step).wait_send())
    for half in range(2):
        each(1, NIN, lambda step: along_copy(half, step).wait_send())
        each(1, NIN, lambda step: weighted_copy(half, z, step).wait_send())
        each(1, NIN, lambda step: predictor_copy(half, step).wait_send())


def per_device(spikes, exposure, weights, direction, residual, iterate):
    table = lag_table()
    lag = jnp.asarray(table, BF16)
    lag_t = jnp.asarray(np.ascontiguousarray(table.T), BF16)
    rows, columns = direction.shape
    vmem = pl.BlockSpec(memory_space=pltpu.VMEM)
    hbm = pl.BlockSpec(memory_space=pl.ANY)
    pair = lambda n: pltpu.SemaphoreType.DMA((2, n))
    scratch = [
        pltpu.VMEM((OWN, NEUR), jnp.int32),
        pltpu.VMEM((BASES * HISTORY, 2 * HISTORY), BF16),
        pltpu.VMEM((2 * HISTORY, BASES * HISTORY), BF16),
        pltpu.VMEM((GROUP, rows, COLS), F32),
        pltpu.VMEM((GROUP, rows, COLS), F32),
        pltpu.VMEM((FEAT, COLS), BF16),
        pltpu.VMEM((FEAT, COLS), F32),
        pltpu.VMEM((FEAT, COLS), BF16),
        pltpu.VMEM((HISTORY + BINS, NEUR), BF16),
        pltpu.VMEM((NEUR, HISTORY + BINS), BF16),
        pltpu.VMEM((BINS, FEAT), BF16),
        pltpu.VMEM((TM, BASES, SLOT, BINS), BF16),
        pltpu.VMEM((GROUP, BASES, SLOT, COLS), BF16),
        pltpu.VMEM((BASES, NEUR, COLS), BF16),
        pltpu.VMEM((8, NIN, 16, COLS), F32),
        pltpu.VMEM((8, NIN, 16, COLS), BF16),
        pltpu.VMEM((8, NIN, 16, COLS), BF16),
        pltpu.VMEM((8, NIN, 16, COLS), F32),
        pltpu.VMEM((8, NIN, 16, COLS), BF16),
        pltpu.VMEM((8, NIN, 16, COLS), BF16),
        pltpu.VMEM((8, NIN, 16, COLS), BF16),
        pltpu.VMEM((TM, rows, COLS), BF16),
        pltpu.VMEM((TM, rows, COLS), BF16),
        pltpu.VMEM((GROUP, rows, COLS), F32),
        pltpu.VMEM((GROUP, 8, COLS), F32),
        pltpu.VMEM((COLS, COLS), F32),
        pltpu.VMEM((8, COLS), F32),
        pltpu.VMEM((TM, 8, COLS), F32),
        pltpu.VMEM((16, COLS), F32),
        pltpu.VMEM((NIN, 16, COLS), F32),
        pltpu.VMEM((8, COLS), F32),
        pltpu.VMEM((TM, 8, COLS), F32),
        pltpu.VMEM((8, COLS), F32),
        pltpu.VMEM((TM, 8, COLS), F32),
        pltpu.VMEM((8, COLS), F32),
        pltpu.VMEM((NIN, 8, COLS), F32),
        pltpu.SemaphoreType.DMA((16,)),
        pair(9), pair(10), pair(GROUP),
        pair(TM), pair(2 * NIN), pair(2 * NIN), pair(2 * NIN), pair(TM),
        pair(TM), pair(NIN), pair(TM), pair(TM), pair(NIN),
    ]
    product, step_size, ratio = pl.pallas_call(
        kernel,
        out_shape=[jax.ShapeDtypeStruct((rows, columns), F32), *[jax.ShapeDtypeStruct((1, columns), F32)] * 2],
        in_specs=[vmem] + [hbm] * 6,
        out_specs=[vmem] * 3,
        scratch_shapes=scratch,
        compiler_params=pltpu.CompilerParams(
            collective_id=0, has_side_effects=True, vmem_limit_bytes=60 * 2**20
        ),
    )(exposure.reshape(2, COLS), spikes, weights, direction, residual, lag, lag_t)
    new_residual = residual - step_size * product
    return iterate + step_size * direction, new_residual, new_residual + ratio * direction


def solution(mesh):
    in_specs = (
        P("tm", "nin"),
        P("tm"),
        P("nin", "nout"),
        P(("nin", "tm"), "nout"),
        P(("nin", "tm"), "nout"),
        P(("nin", "tm"), "nout"),
    )
    out_specs = (P(("nin", "tm"), "nout"), P(("nin", "tm"), "nout"), P(("nin", "tm"), "nout"))
    return jax.shard_map(
        per_device, mesh=mesh, in_specs=in_specs, out_specs=out_specs, check_vma=False
    )
```

```python
import functools
import math

import jax
import jax.numpy as jnp
import numpy as np
from jax import lax
from jax.experimental import pallas as pl
from jax.experimental.pallas import tpu as pltpu
from jax.sharding import PartitionSpec as P

BASES = 8
HISTORY = 128
RIDGE_WEIGHT = 0.05
NORM_EPS = 1e-06
MESH = pl.DeviceIdType.MESH
F32 = jnp.float32
BF16 = jnp.bfloat16

TM = 16
NIN = 8
NOUT = 4
EARLY = 3
GROUP = 4
BINS = 1024
OWN = 256
NEUR = 256
COLS = 128
FEAT = NEUR * BASES
SLOT = NEUR // TM


def basis_table():
    lag_values = np.arange(1, HISTORY + 1, dtype=np.float32)
    warped = np.log(lag_values + np.float32(1.0))
    log_low = math.log(2.0)
    log_high = math.log(HISTORY + 1.0)
    spacing = (log_high - log_low) / (BASES - 1)
    centers = np.float32(log_low) + np.float32(spacing) * np.arange(BASES, dtype=np.float32)
    phases = (warped[:, None] - centers[None, :]) * np.float32(math.pi / (2.0 * spacing))
    phases = np.clip(phases, np.float32(-math.pi), np.float32(math.pi))
    bumps = np.float32(0.5) * (np.float32(1.0) + np.cos(phases))
    bumps = bumps / np.sum(bumps, axis=0, keepdims=True)
    return bumps.astype(np.float32)


def lag_table():
    basis = basis_table()
    lag = np.arange(HISTORY)[:, None] + HISTORY - np.arange(2 * HISTORY)[None, :]
    valid = (lag >= 1) & (lag <= HISTORY)
    table = np.where(valid[None], basis.T[:, np.clip(lag - 1, 0, HISTORY - 1)], np.float32(0.0))
    return table.reshape(BASES * HISTORY, 2 * HISTORY)


def kernel(
    exposure_ref, spikes_hbm, weights_hbm, direction_hbm, residual_hbm, lag_hbm, lag_t_hbm,
    product_out, step_out, ratio_out,
    spikes_in, lag, lag_t, d32, r32, w16, w32, wp, spk, spk_t, x, xt,
    d_send, d_all, p_own, p_send, p_recv, a_own, a_send, a_recv, wt_all, g_send, g_recv, g_nat,
    ticks, ticks_t, nd_send, nd_recv, cv_send, cv_recv, c2_send, c2_recv, nn_send, nn_recv, nz_send, nz_recv,
    load_sem, on_sem, spk_sem, halo_sem, tick_sem, d_sem, p_sem, a_sem, wt_sem, g_sem, nd_sem, cv_sem, c2_sem, nn_sem, nz_sem,
):
    me = lax.axis_index("tm")
    z = lax.axis_index("nin")
    xo = lax.axis_index("nout")
    team = me // GROUP
    part = lax.rem(me, GROUP)

    def tm_peer(step):
        return lax.rem(me + step, TM)

    def z_peer(step):
        return lax.rem(z + step, NIN)

    def team_peer(step):
        return team * GROUP + lax.rem(part + step, GROUP)

    chip = me // 2
    core = lax.rem(me, 2)
    half_own = lax.rem(chip, 2)
    mate = chip + 1 - 2 * half_own

    def at(dy, c):
        return lax.rem(chip + dy + TM // 2, TM // 2) * 2 + c

    def ahead(peer):
        return lax.rem(peer + TM - me, TM)

    def behind(peer):
        return lax.rem(me + TM - peer, TM)

    def x_peer(step):
        return lax.rem(xo + step, NOUT)

    def swing(turn, middle):
        return middle + (1 - 2 * lax.rem(turn, 2)) * ((turn + 1) // 2)

    def remote(src, dst, sems, slot, tm_index, z_index, x_index=None):
        return pltpu.make_async_remote_copy(
            src_ref=src, dst_ref=dst, send_sem=sems.at[0, slot], recv_sem=sems.at[1, slot],
            device_id=(tm_index, z_index, xo if x_index is None else x_index), device_id_type=MESH,
        )

    def far_first(count, body):
        each(0, count - 1, lambda turn: body(swing(turn, count // 2)))

    def each(first, last, body):
        def run(step, carry):
            body(step)
            return carry

        lax.fori_loop(first, last, run, 0)

    loads = [
        pltpu.make_async_copy(spikes_hbm, spikes_in, load_sem.at[0]),
        pltpu.make_async_copy(lag_hbm, lag, load_sem.at[1]),
        pltpu.make_async_copy(lag_t_hbm, lag_t, load_sem.at[2]),
        pltpu.make_async_copy(
            weights_hbm.at[:, pl.ds(pl.multiple_of(part * COLS, COLS), COLS)], w16, load_sem.at[3]
        ),
    ]
    blocks = [
        [
            pltpu.make_async_copy(source.at[:, k * COLS : (k + 1) * COLS], target.at[k], load_sem.at[4 + 4 * n + k])
            for k in range(GROUP)
        ]
        for n, (source, target) in enumerate(((direction_hbm, d32), (residual_hbm, r32)))
    ]
    for copy in blocks[0] + loads[:1]:
        copy.start()

    barrier = pltpu.get_barrier_semaphore()

    def greet_tm(step):
        pl.semaphore_signal(barrier, inc=1, device_id=(tm_peer(step), z, xo), device_id_type=MESH)

    def greet_z(step):
        pl.semaphore_signal(barrier, inc=1, device_id=(me, z_peer(step), xo), device_id_type=MESH)

    far_first(TM, greet_tm)
    far_first(NIN, greet_z)

    def greet_x(step):
        for c in range(2):
            pl.semaphore_signal(
                barrier, inc=1, device_id=(chip * 2 + c, z, x_peer(step)), device_id_type=MESH
            )

    each(1, NOUT, greet_x)
    for copy in loads[1:] + blocks[1]:
        copy.start()

    for copy in blocks[0]:
        copy.wait()
    for k in range(GROUP):
        for b in range(BASES):
            d_send[k, b] = d32[k, pl.ds(b, SLOT, stride=BASES), :].astype(BF16)
    loads[0].wait()
    own_rows = pl.ds(pl.multiple_of(HISTORY + part * OWN, HISTORY), OWN)
    spk[own_rows, :] = spikes_in[...].astype(F32).astype(BF16)
    ticks[part, 0:2, :] = exposure_ref[...].astype(F32) / 8.0
    ticks[part, 2:8, :] = jnp.zeros((6, COLS), F32)
    pl.semaphore_wait(barrier, TM - 1 + NIN - 1 + 2 * (NOUT - 1))

    def core_copy():
        return remote(spk.at[own_rows], spk.at[own_rows], spk_sem, 8, chip * 2 + 1 - core, z)

    def core_arrival():
        rows = pl.ds(pl.multiple_of(HISTORY + (half_own * 2 + 1 - core) * OWN, HISTORY), OWN)
        return remote(spk.at[rows], spk.at[rows], spk_sem, 8, chip * 2 + 1 - core, z)

    def quarter(half, from_core, x_index):
        return pl.ds(pl.multiple_of(HISTORY + (half * 2 + from_core) * OWN + x_index * 64, 64), 64)

    def mate_copy():
        rows = quarter(half_own, core, xo)
        return remote(spk.at[rows], spk.at[rows], spk_sem, 0, mate * 2 + core, z)

    def mate_arrival(step, other):
        from_core = core if other == 0 else 1 - core
        rows = quarter(1 - half_own, from_core, x_peer(NOUT - step))
        return remote(spk.at[rows], spk.at[rows], spk_sem, step * 2 + other, me, z)

    def spread_copy(step, other):
        rows = quarter(1 - half_own, core, xo)
        to_core = core if other == 0 else 1 - core
        return remote(spk.at[rows], spk.at[rows], spk_sem, step * 2 + other, chip * 2 + to_core, z, x_peer(step))

    def halo_copy(k):
        rows = pl.ds(pl.multiple_of(BINS + xo * 32, 32), 32)
        return remote(
            spk.at[rows], spk.at[halo_rows(xo)], halo_sem, 8 + k, lax.rem((team + 1) * GROUP + 2 * k + 1, TM), z
        )

    def halo_rows(x_index):
        return pl.ds(pl.multiple_of(x_index * 32, 32), 32)

    def halo_first():
        rows = halo_rows(xo)
        return remote(spk.at[rows], spk.at[rows], halo_sem, 8 + half_own, me, z)

    def halo_spread(step, other):
        rows = halo_rows(xo)
        return remote(spk.at[rows], spk.at[rows], halo_sem, step * 2 + other, chip * 2 + 1 - other, z, x_peer(step))

    def halo_arrival(step):
        rows = halo_rows(x_peer(NOUT - step))
        return remote(spk.at[rows], spk.at[rows], halo_sem, step * 2 + 1 - core, me, z)

    def tick_copy(step):
        return remote(ticks.at[part], ticks.at[part], tick_sem, step, team_peer(step), z)

    def tick_arrival(step):
        slot = lax.rem(part + GROUP - step, GROUP)
        return remote(ticks.at[slot], ticks.at[slot], tick_sem, step, team_peer(step), z)

    d_rows = pl.ds(pl.multiple_of(me * SLOT, SLOT), SLOT)

    def direction_copy(step):
        peer = tm_peer(step)
        return remote(d_send.at[lax.rem(peer, GROUP)], d_all.at[:, d_rows, :], d_sem, step, peer, z)

    def direction_arrival(step):
        rows = pl.ds(pl.multiple_of(tm_peer(TM - step) * SLOT, SLOT), SLOT)
        return remote(d_send.at[0], d_all.at[:, rows, :], d_sem, step, tm_peer(step), z)

    onward = [(-1, 0, 2), (1, 0, -2), (-1, 1, 2), (1, 1, -2), (-2, 0, 2), (2, 1, -2)]

    def direction_onward(n):
        dy, c, to = onward[n]
        origin, target = at(dy, c), at(to, core)
        rows = pl.ds(pl.multiple_of(origin * SLOT, SLOT), SLOT)
        return pltpu.make_async_remote_copy(
            src_ref=d_all.at[:, rows, :], dst_ref=d_all.at[:, rows, :], send_sem=on_sem.at[n],
            recv_sem=d_sem.at[1, lax.rem(target + TM - origin, TM)], device_id=(target, z, xo), device_id_type=MESH,
        )

    sends_halo = jnp.logical_and(part == GROUP - 1, team < TM // GROUP - 1)
    hands_halo = jnp.logical_and(core == 1, team > 0)
    spreads = [(step, other) for step in (2, 1, 3, 0) for other in range(2) if (step, other) != (0, 0)]

    mate_copy().start()

    @pl.when(sends_halo)
    def _():
        halo_copy(0).start()
        halo_copy(1).start()

    core_copy().start()
    near = [(dy, c) for dy in (1, -1, 2, -2) for c in range(2)]
    for dy, c in near:
        direction_copy(ahead(at(dy, c))).start()
    direction_copy(ahead(at(0, 1 - core))).start()
    each(1, GROUP, lambda step: tick_copy(step).start())
    d_all[:, d_rows, :] = d_send[part]

    loads[3].wait()
    w32[...] = w16[...].astype(F32)
    for b in range(BASES):
        wp[b * NEUR : (b + 1) * NEUR, :] = w32[pl.ds(b, NEUR, stride=BASES), :].astype(BF16)

    def turn_spikes(n):
        rows = pl.ds(pl.multiple_of(n * HISTORY, HISTORY), HISTORY)
        spk_t[:, rows] = spk[rows, :].astype(F32).T.astype(BF16)

    own_first = half_own * 4 + 1

    def features(k):
        block = lax.rem(own_first + k, 8)
        rows = pl.ds(pl.multiple_of(k * HISTORY, HISTORY), HISTORY)
        window = pl.ds(pl.multiple_of(block * HISTORY, HISTORY), 2 * HISTORY)
        made = jnp.dot(lag[...], spk[window, :], preferred_element_type=F32)
        for b in range(BASES):
            x[rows, b * NEUR : (b + 1) * NEUR] = made[b * HISTORY : (b + 1) * HISTORY].astype(BF16)
        made_t = jnp.dot(spk_t[:, window], lag_t[...], preferred_element_type=F32)
        for b in range(BASES):
            piece = made_t[:, b * HISTORY : (b + 1) * HISTORY].astype(BF16)
            xt[:, b, :, rows] = piece.reshape(TM, SLOT, HISTORY)

    loads[1].wait()
    loads[2].wait()
    core_arrival().wait_recv()
    each(0, 4, lambda k: turn_spikes(own_first + k))
    each(0, EARLY, features)

    mate_arrival(0, 0).wait_recv()
    for step, other in spreads:
        spread_copy(step, other).start()

    @pl.when(team == 0)
    def _():
        spk[0:HISTORY, :] = jnp.zeros((HISTORY, NEUR), BF16)

    @pl.when(hands_halo)
    def _():
        halo_first().wait_recv()
        for step, other in spreads:
            halo_spread(step, other).start()

    for n, (dy, c, to) in enumerate(onward):
        direction_arrival(behind(at(dy, c))).wait_recv()
        direction_onward(n).start()

    def predictor(first, last):
        made = jnp.dot(x[first * HISTORY : last * HISTORY, :], wp[...], preferred_element_type=F32)
        made = made.reshape(last - first, NIN, 16, COLS)
        p_own[first:last] = made
        p_send[first:last] = made.astype(BF16)

    def predictor_copy(late, step):
        blocks_of = slice(EARLY, 8) if late else slice(0, EARLY)
        return remote(
            p_send.at[blocks_of, z_peer(step)], p_recv.at[blocks_of, step], p_sem, late * NIN + step, me, z_peer(step)
        )

    predictor(0, EARLY)
    far_first(NIN, lambda step: predictor_copy(0, step).start())

    for copy in blocks[1]:
        copy.wait()
    for k in range(GROUP):
        nd_send[k : k + 1, :] = jnp.sum(r32[k] * r32[k], axis=0, keepdims=True)
        nd_send[GROUP + k : GROUP + k + 1, :] = jnp.sum(d32[k] * d32[k], axis=0, keepdims=True)

    def nd_copy(step):
        return remote(nd_send, nd_recv.at[step], nd_sem, step, tm_peer(step), z)

    each(1, TM, lambda step: nd_copy(step).start())

    for step, other in spreads:
        mate_arrival(step, other).wait_recv()

    @pl.when(team > 0)
    def _():
        each(core, NOUT, lambda step: halo_arrival(step).wait_recv())

    each(0, 5, lambda k: turn_spikes(lax.rem(own_first + 4 + k, 9)))
    each(EARLY, 8, features)
    predictor(EARLY, 8)
    far_first(NIN, lambda step: predictor_copy(1, step).start())

    direction_arrival(behind(at(0, 1 - core))).wait_recv()
    for dy, c in ((-2, 1), (2, 0), (3, 0), (3, 1), (-3, 0), (-3, 1), (4, 0), (4, 1)):
        direction_arrival(behind(at(dy, c))).wait_recv()

    def along_copy(half, step):
        blocks_of = slice(half * 4, half * 4 + 4)
        return remote(
            a_send.at[blocks_of, z_peer(step)], a_recv.at[blocks_of, step], a_sem, half * NIN + step, me, z_peer(step)
        )

    for half in range(2):
        made = jnp.dot(
            x[half * 512 : half * 512 + 512, :], d_all[...].reshape(FEAT, COLS), preferred_element_type=F32
        ).reshape(4, NIN, 16, COLS)
        a_own[half * 4 : half * 4 + 4] = made
        a_send[half * 4 : half * 4 + 4] = made.astype(BF16)
        far_first(NIN, lambda step: along_copy(half, step).start())

    each(1, GROUP, lambda step: tick_arrival(step).wait_recv())
    table = jnp.concatenate([ticks[k, 0:2, :] for k in range(GROUP)] + [jnp.zeros((COLS - 8, COLS), F32)], axis=0)
    ticks_t[...] = table.T
    tick_rows = ticks_t[pl.ds(pl.multiple_of(z * 16, 16), 16), :]
    lane = lax.broadcasted_iota(jnp.int32, (16, COLS), 1)

    each(1, TM, lambda step: nd_copy(step).wait_recv())
    cv_send[0:8, :] = nd_send[...] + jnp.sum(nd_recv[1:TM], axis=0)

    for late in range(2):
        each(1, NIN, lambda step: predictor_copy(late, step).wait_recv())

    def weighted_copy(half, slot, step):
        place = wt_all.at[slice(half * 4, half * 4 + 4), slot]
        return remote(place, place, wt_sem, half * NIN + step, me, z_peer(step))

    curvature_part = jnp.zeros((1, COLS), F32)
    for half in range(2):
        each(1, NIN, lambda step: along_copy(half, step).wait_recv())
        for k in range(half * 4, half * 4 + 4):
            p_sum = p_own[k, z]
            a_sum = a_own[k, z]
            for step in range(1, NIN):
                p_sum += p_recv[k, step].astype(F32)
                a_sum += a_recv[k, step].astype(F32)
            scale = jnp.sum(jnp.where(lane == lax.rem(own_first + k, 8), tick_rows, 0.0), axis=1, keepdims=True)
            weighted = ((scale * jnp.exp(p_sum)) * a_sum).astype(BF16)
            wt_all[k, z] = weighted
            curvature_part += jnp.sum(weighted.astype(F32) * a_sum, axis=0, keepdims=True)
        far_first(NIN, lambda step: weighted_copy(half, z, step).start())
    cv_send[8:16, :] = jnp.concatenate([curvature_part, jnp.zeros((7, COLS), F32)], axis=0)

    def cv_copy(step):
        return remote(cv_send, cv_recv.at[step], cv_sem, step, me, z_peer(step))

    each(1, NIN, lambda step: cv_copy(step).start())

    for half in range(2):
        each(1, NIN, lambda step: weighted_copy(half, z_peer(NIN - step), step).wait_recv())

    def gram_copy(step):
        return remote(g_send.at[tm_peer(step)], g_recv.at[me], g_sem, step, tm_peer(step), z)

    def gram_to(peer):
        return remote(g_send.at[peer], g_recv.at[me], g_sem, lax.rem(peer + TM - me, TM), peer, z)

    def gram_arrival(step):
        return remote(g_send.at[0], g_recv.at[tm_peer(TM - step)], g_sem, step, tm_peer(step), z)

    def gram(turn):
        group = lax.rem(team + swing(turn, 2), GROUP)
        rows = pl.ds(group * 4, 4)
        made = jnp.dot(
            xt[rows].reshape(4 * SLOT * BASES, BINS), wt_all[...].reshape(BINS, COLS), preferred_element_type=F32
        )
        g_send[rows] = made.astype(BF16).reshape(4, SLOT * BASES, COLS)

        @pl.when(turn < 3)
        def _():
            each(0, GROUP, lambda k: gram_to(group * GROUP + k).start())

    each(0, 4, gram)
    each(1, GROUP, lambda step: gram_to(team_peer(step)).start())
    g_recv[me] = g_send[me]

    each(1, NIN, lambda step: cv_copy(step).wait_recv())
    cv_sum = cv_send[...] + jnp.sum(cv_recv[1:NIN], axis=0)
    old_norm = cv_sum[0:4, :]
    c2_send[...] = cv_sum[8:16, :]
    c2_recv[me] = cv_sum[8:16, :]

    def c2_copy(step):
        return remote(c2_send, c2_recv.at[me], c2_sem, step, tm_peer(step), z)

    def c2_arrival(step):
        return remote(c2_send, c2_recv.at[tm_peer(TM - step)], c2_sem, step, tm_peer(step), z)

    each(1, TM, lambda step: c2_copy(step).start())
    each(1, TM, lambda step: c2_arrival(step).wait_recv())
    step_sizes = []
    for k in range(GROUP):
        total = c2_recv[k, 0:1, :]
        for t in range(1, TM // GROUP):
            total += c2_recv[t * GROUP + k, 0:1, :]
        curvature = total / (BINS * (TM // GROUP)) + RIDGE_WEIGHT * cv_sum[4 + k : 5 + k, :]
        step_size = old_norm[k : k + 1, :] / curvature
        step_sizes.append(step_size)
        step_out[:, k * COLS : (k + 1) * COLS] = step_size

    each(1, TM, lambda step: gram_arrival(step).wait_recv())
    nn_send[4:8, :] = jnp.zeros((4, COLS), F32)
    for k in range(GROUP):
        total = g_recv[k].astype(F32)
        for t in range(1, TM // GROUP):
            total += g_recv[t * GROUP + k].astype(F32)
        for b in range(BASES):
            g_nat[k, pl.ds(b, SLOT, stride=BASES), :] = total[b * SLOT : (b + 1) * SLOT]
        product = g_nat[k] / (BINS * (TM // GROUP)) + RIDGE_WEIGHT * d32[k]
        new_residual = r32[k] - step_sizes[k] * product
        product_out[:, k * COLS : (k + 1) * COLS] = product
        nn_send[k : k + 1, :] = jnp.sum(new_residual * new_residual, axis=0, keepdims=True)

    def nn_copy(step):
        return remote(nn_send, nn_recv.at[step], nn_sem, step, tm_peer(step), z)

    far_first(TM, lambda step: nn_copy(step).start())
    each(1, TM, lambda step: nn_copy(step).wait_recv())
    nz_send[...] = nn_send[...] + jnp.sum(nn_recv[1:TM], axis=0)

    def nz_copy(step):
        return remote(nz_send, nz_recv.at[step], nz_sem, step, me, z_peer(step))

    far_first(NIN, lambda step: nz_copy(step).start())
    each(1, NIN, lambda step: nz_copy(step).wait_recv())
    new_norm = nz_send[...] + jnp.sum(nz_recv[1:NIN], axis=0)
    for k in range(GROUP):
        ratio = new_norm[k : k + 1, :] / (old_norm[k : k + 1, :] + NORM_EPS)
        ratio_out[:, k * COLS : (k + 1) * COLS] = ratio

    mate_copy().wait_send()
    core_copy().wait_send()
    for step, other in spreads:
        spread_copy(step, other).wait_send()

    @pl.when(sends_halo)
    def _():
        halo_copy(0).wait_send()
        halo_copy(1).wait_send()

    @pl.when(hands_halo)
    def _():
        for step, other in spreads:
            halo_spread(step, other).wait_send()

    each(1, GROUP, lambda step: tick_copy(step).wait_send())
    for dy, c in near:
        direction_copy(ahead(at(dy, c))).wait_send()
    direction_copy(ahead(at(0, 1 - core))).wait_send()
    for n in range(len(onward)):
        direction_onward(n).wait_send()
    for copy in (nd_copy, gram_copy, c2_copy, nn_copy):
        each(1, TM, lambda step: copy(step).wait_send())
    for copy in (cv_copy, nz_copy):
        each(1, NIN, lambda step: copy(step).wait_send())
    for half in range(2):
        each(1, NIN, lambda step: along_copy(half, step).wait_send())
        each(1, NIN, lambda step: weighted_copy(half, z, step).wait_send())
        each(1, NIN, lambda step: predictor_copy(half, step).wait_send())


def per_device(spikes, exposure, weights, direction, residual, iterate):
    table = lag_table()
    lag = jnp.asarray(table, BF16)
    lag_t = jnp.asarray(np.ascontiguousarray(table.T), BF16)
    rows, columns = direction.shape
    vmem = pl.BlockSpec(memory_space=pltpu.VMEM)
    hbm = pl.BlockSpec(memory_space=pl.ANY)
    pair = lambda n: pltpu.SemaphoreType.DMA((2, n))
    scratch = [
        pltpu.VMEM((OWN, NEUR), jnp.int32),
        pltpu.VMEM((BASES * HISTORY, 2 * HISTORY), BF16),
        pltpu.VMEM((2 * HISTORY, BASES * HISTORY), BF16),
        pltpu.VMEM((GROUP, rows, COLS), F32),
        pltpu.VMEM((GROUP, rows, COLS), F32),
        pltpu.VMEM((FEAT, COLS), BF16),
        pltpu.VMEM((FEAT, COLS), F32),
        pltpu.VMEM((FEAT, COLS), BF16),
        pltpu.VMEM((HISTORY + BINS, NEUR), BF16),
        pltpu.VMEM((NEUR, HISTORY + BINS), BF16),
        pltpu.VMEM((BINS, FEAT), BF16),
        pltpu.VMEM((TM, BASES, SLOT, BINS), BF16),
        pltpu.VMEM((GROUP, BASES, SLOT, COLS), BF16),
        pltpu.VMEM((BASES, NEUR, COLS), BF16),
        pltpu.VMEM((8, NIN, 16, COLS), F32),
        pltpu.VMEM((8, NIN, 16, COLS), BF16),
        pltpu.VMEM((8, NIN, 16, COLS), BF16),
        pltpu.VMEM((8, NIN, 16, COLS), F32),
        pltpu.VMEM((8, NIN, 16, COLS), BF16),
        pltpu.VMEM((8, NIN, 16, COLS), BF16),
        pltpu.VMEM((8, NIN, 16, COLS), BF16),
        pltpu.VMEM((TM, rows, COLS), BF16),
        pltpu.VMEM((TM, rows, COLS), BF16),
        pltpu.VMEM((GROUP, rows, COLS), F32),
        pltpu.VMEM((GROUP, 8, COLS), F32),
        pltpu.VMEM((COLS, COLS), F32),
        pltpu.VMEM((8, COLS), F32),
        pltpu.VMEM((TM, 8, COLS), F32),
        pltpu.VMEM((16, COLS), F32),
        pltpu.VMEM((NIN, 16, COLS), F32),
        pltpu.VMEM((8, COLS), F32),
        pltpu.VMEM((TM, 8, COLS), F32),
        pltpu.VMEM((8, COLS), F32),
        pltpu.VMEM((TM, 8, COLS), F32),
        pltpu.VMEM((8, COLS), F32),
        pltpu.VMEM((NIN, 8, COLS), F32),
        pltpu.SemaphoreType.DMA((16,)),
        pltpu.SemaphoreType.DMA((6,)),
        pair(9), pair(10), pair(GROUP),
        pair(TM), pair(2 * NIN), pair(2 * NIN), pair(2 * NIN), pair(TM),
        pair(TM), pair(NIN), pair(TM), pair(TM), pair(NIN),
    ]
    product, step_size, ratio = pl.pallas_call(
        kernel,
        out_shape=[jax.ShapeDtypeStruct((rows, columns), F32), *[jax.ShapeDtypeStruct((1, columns), F32)] * 2],
        in_specs=[vmem] + [hbm] * 6,
        out_specs=[vmem] * 3,
        scratch_shapes=scratch,
        compiler_params=pltpu.CompilerParams(
            collective_id=0, has_side_effects=True, vmem_limit_bytes=60 * 2**20
        ),
    )(exposure.reshape(2, COLS), spikes, weights, direction, residual, lag, lag_t)
    new_residual = residual - step_size * product
    return iterate + step_size * direction, new_residual, new_residual + ratio * direction


def solution(mesh):
    in_specs = (
        P("tm", "nin"),
        P("tm"),
        P("nin", "nout"),
        P(("nin", "tm"), "nout"),
        P(("nin", "tm"), "nout"),
        P(("nin", "tm"), "nout"),
    )
    out_specs = (P(("nin", "tm"), "nout"), P(("nin", "tm"), "nout"), P(("nin", "tm"), "nout"))
    return jax.shard_map(
        per_device, mesh=mesh, in_specs=in_specs, out_specs=out_specs, check_vma=False
    )
```

```python
import functools
import math

import jax
import jax.numpy as jnp
import numpy as np
from jax import lax
from jax.experimental import pallas as pl
from jax.experimental.pallas import tpu as pltpu
from jax.sharding import PartitionSpec as P

BASES = 8
HISTORY = 128
RIDGE_WEIGHT = 0.05
NORM_EPS = 1e-06
MESH = pl.DeviceIdType.MESH
F32 = jnp.float32
BF16 = jnp.bfloat16

TM = 16
NIN = 8
NOUT = 4
EARLY = 3
GROUP = 4
BINS = 1024
OWN = 256
NEUR = 256
COLS = 128
FEAT = NEUR * BASES
SLOT = NEUR // TM


def basis_table():
    lag_values = np.arange(1, HISTORY + 1, dtype=np.float32)
    warped = np.log(lag_values + np.float32(1.0))
    log_low = math.log(2.0)
    log_high = math.log(HISTORY + 1.0)
    spacing = (log_high - log_low) / (BASES - 1)
    centers = np.float32(log_low) + np.float32(spacing) * np.arange(BASES, dtype=np.float32)
    phases = (warped[:, None] - centers[None, :]) * np.float32(math.pi / (2.0 * spacing))
    phases = np.clip(phases, np.float32(-math.pi), np.float32(math.pi))
    bumps = np.float32(0.5) * (np.float32(1.0) + np.cos(phases))
    bumps = bumps / np.sum(bumps, axis=0, keepdims=True)
    return bumps.astype(np.float32)


def lag_table():
    basis = basis_table()
    lag = np.arange(HISTORY)[:, None] + HISTORY - np.arange(2 * HISTORY)[None, :]
    valid = (lag >= 1) & (lag <= HISTORY)
    table = np.where(valid[None], basis.T[:, np.clip(lag - 1, 0, HISTORY - 1)], np.float32(0.0))
    return table.reshape(BASES * HISTORY, 2 * HISTORY)


def kernel(
    exposure_ref, spikes_hbm, weights_hbm, direction_hbm, residual_hbm, lag_hbm, lag_t_hbm,
    product_out, step_out, ratio_out,
    spikes_in, lag, lag_t, d32, r32, w16, w32, wp, spk, spk_t, x, xt,
    d_send, d_all, p_own, p_send, p_recv, a_own, a_send, a_recv, wt_all, g_send, g_recv, h_recv, g_nat,
    ticks, ticks_t, nd_send, nd_recv, cv_send, cv_recv, c2_send, c2_recv, nn_send, nn_recv, nz_send, nz_recv,
    load_sem, on_sem, spk_sem, halo_sem, tick_sem, d_sem, p_sem, a_sem, wt_sem, g_sem, h_sem, nd_sem, cv_sem, c2_sem, nn_sem, nz_sem,
):
    me = lax.axis_index("tm")
    z = lax.axis_index("nin")
    xo = lax.axis_index("nout")
    team = me // GROUP
    part = lax.rem(me, GROUP)

    def tm_peer(step):
        return lax.rem(me + step, TM)

    def z_peer(step):
        return lax.rem(z + step, NIN)

    def team_peer(step):
        return team * GROUP + lax.rem(part + step, GROUP)

    chip = me // 2
    core = lax.rem(me, 2)
    half_own = lax.rem(chip, 2)
    mate = chip + 1 - 2 * half_own

    def at(dy, c):
        return lax.rem(chip + dy + TM // 2, TM // 2) * 2 + c

    def ahead(peer):
        return lax.rem(peer + TM - me, TM)

    def behind(peer):
        return lax.rem(me + TM - peer, TM)

    def x_peer(step):
        return lax.rem(xo + step, NOUT)

    def swing(turn, middle):
        return middle + (1 - 2 * lax.rem(turn, 2)) * ((turn + 1) // 2)

    def remote(src, dst, sems, slot, tm_index, z_index, x_index=None):
        return pltpu.make_async_remote_copy(
            src_ref=src, dst_ref=dst, send_sem=sems.at[0, slot], recv_sem=sems.at[1, slot],
            device_id=(tm_index, z_index, xo if x_index is None else x_index), device_id_type=MESH,
        )

    def far_first(count, body):
        each(0, count - 1, lambda turn: body(swing(turn, count // 2)))

    def each(first, last, body):
        def run(step, carry):
            body(step)
            return carry

        lax.fori_loop(first, last, run, 0)

    loads = [
        pltpu.make_async_copy(spikes_hbm, spikes_in, load_sem.at[0]),
        pltpu.make_async_copy(lag_hbm, lag, load_sem.at[1]),
        pltpu.make_async_copy(lag_t_hbm, lag_t, load_sem.at[2]),
        pltpu.make_async_copy(
            weights_hbm.at[:, pl.ds(pl.multiple_of(part * COLS, COLS), COLS)], w16, load_sem.at[3]
        ),
    ]
    blocks = [
        [
            pltpu.make_async_copy(source.at[:, k * COLS : (k + 1) * COLS], target.at[k], load_sem.at[4 + 4 * n + k])
            for k in range(GROUP)
        ]
        for n, (source, target) in enumerate(((direction_hbm, d32), (residual_hbm, r32)))
    ]
    for copy in blocks[0] + loads[:1]:
        copy.start()

    barrier = pltpu.get_barrier_semaphore()

    def greet_tm(step):
        pl.semaphore_signal(barrier, inc=1, device_id=(tm_peer(step), z, xo), device_id_type=MESH)

    def greet_z(step):
        pl.semaphore_signal(barrier, inc=1, device_id=(me, z_peer(step), xo), device_id_type=MESH)

    far_first(TM, greet_tm)
    far_first(NIN, greet_z)

    def greet_x(step):
        for c in range(2):
            pl.semaphore_signal(
                barrier, inc=1, device_id=(chip * 2 + c, z, x_peer(step)), device_id_type=MESH
            )

    each(1, NOUT, greet_x)
    for copy in loads[1:] + blocks[1]:
        copy.start()

    for copy in blocks[0]:
        copy.wait()
    for k in range(GROUP):
        for b in range(BASES):
            d_send[k, b] = d32[k, pl.ds(b, SLOT, stride=BASES), :].astype(BF16)
    loads[0].wait()
    own_rows = pl.ds(pl.multiple_of(HISTORY + part * OWN, HISTORY), OWN)
    spk[own_rows, :] = spikes_in[...].astype(F32).astype(BF16)
    ticks[part, 0:2, :] = exposure_ref[...].astype(F32) / 8.0
    ticks[part, 2:8, :] = jnp.zeros((6, COLS), F32)
    pl.semaphore_wait(barrier, TM - 1 + NIN - 1 + 2 * (NOUT - 1))

    def core_copy():
        return remote(spk.at[own_rows], spk.at[own_rows], spk_sem, 8, chip * 2 + 1 - core, z)

    def core_arrival():
        rows = pl.ds(pl.multiple_of(HISTORY + (half_own * 2 + 1 - core) * OWN, HISTORY), OWN)
        return remote(spk.at[rows], spk.at[rows], spk_sem, 8, chip * 2 + 1 - core, z)

    def quarter(half, from_core, x_index):
        return pl.ds(pl.multiple_of(HISTORY + (half * 2 + from_core) * OWN + x_index * 64, 64), 64)

    def mate_copy():
        rows = quarter(half_own, core, xo)
        return remote(spk.at[rows], spk.at[rows], spk_sem, 0, mate * 2 + core, z)

    def mate_arrival(step, other):
        from_core = core if other == 0 else 1 - core
        rows = quarter(1 - half_own, from_core, x_peer(NOUT - step))
        return remote(spk.at[rows], spk.at[rows], spk_sem, step * 2 + other, me, z)

    def spread_copy(step, other):
        rows = quarter(1 - half_own, core, xo)
        to_core = core if other == 0 else 1 - core
        return remote(spk.at[rows], spk.at[rows], spk_sem, step * 2 + other, chip * 2 + to_core, z, x_peer(step))

    def halo_copy(k):
        rows = pl.ds(pl.multiple_of(BINS + xo * 32, 32), 32)
        return remote(
            spk.at[rows], spk.at[halo_rows(xo)], halo_sem, 8 + k, lax.rem((team + 1) * GROUP + 2 * k + 1, TM), z
        )

    def halo_rows(x_index):
        return pl.ds(pl.multiple_of(x_index * 32, 32), 32)

    def halo_first():
        rows = halo_rows(xo)
        return remote(spk.at[rows], spk.at[rows], halo_sem, 8 + half_own, me, z)

    def halo_spread(step, other):
        rows = halo_rows(xo)
        return remote(spk.at[rows], spk.at[rows], halo_sem, step * 2 + other, chip * 2 + 1 - other, z, x_peer(step))

    def halo_arrival(step):
        rows = halo_rows(x_peer(NOUT - step))
        return remote(spk.at[rows], spk.at[rows], halo_sem, step * 2 + 1 - core, me, z)

    def tick_copy(step):
        return remote(ticks.at[part], ticks.at[part], tick_sem, step, team_peer(step), z)

    def tick_arrival(step):
        slot = lax.rem(part + GROUP - step, GROUP)
        return remote(ticks.at[slot], ticks.at[slot], tick_sem, step, team_peer(step), z)

    d_rows = pl.ds(pl.multiple_of(me * SLOT, SLOT), SLOT)

    def direction_copy(step):
        peer = tm_peer(step)
        return remote(d_send.at[lax.rem(peer, GROUP)], d_all.at[:, d_rows, :], d_sem, step, peer, z)

    def direction_arrival(step):
        rows = pl.ds(pl.multiple_of(tm_peer(TM - step) * SLOT, SLOT), SLOT)
        return remote(d_send.at[0], d_all.at[:, rows, :], d_sem, step, tm_peer(step), z)

    onward = [(-1, 0, 2), (1, 0, -2), (-1, 1, 2), (1, 1, -2), (-2, 0, 2), (2, 1, -2)]

    def direction_onward(n):
        dy, c, to = onward[n]
        origin, target = at(dy, c), at(to, core)
        rows = pl.ds(pl.multiple_of(origin * SLOT, SLOT), SLOT)
        return pltpu.make_async_remote_copy(
            src_ref=d_all.at[:, rows, :], dst_ref=d_all.at[:, rows, :], send_sem=on_sem.at[n],
            recv_sem=d_sem.at[1, lax.rem(target + TM - origin, TM)], device_id=(target, z, xo), device_id_type=MESH,
        )

    sends_halo = jnp.logical_and(part == GROUP - 1, team < TM // GROUP - 1)
    hands_halo = jnp.logical_and(core == 1, team > 0)
    spreads = [(step, other) for step in (2, 1, 3, 0) for other in range(2) if (step, other) != (0, 0)]

    mate_copy().start()

    @pl.when(sends_halo)
    def _():
        halo_copy(0).start()
        halo_copy(1).start()

    core_copy().start()
    near = [(dy, c) for dy in (1, -1, 2, -2) for c in range(2)]
    for dy, c in near:
        direction_copy(ahead(at(dy, c))).start()
    direction_copy(ahead(at(0, 1 - core))).start()
    each(1, GROUP, lambda step: tick_copy(step).start())
    d_all[:, d_rows, :] = d_send[part]

    loads[3].wait()
    w32[...] = w16[...].astype(F32)
    for b in range(BASES):
        wp[b * NEUR : (b + 1) * NEUR, :] = w32[pl.ds(b, NEUR, stride=BASES), :].astype(BF16)

    def turn_spikes(n):
        rows = pl.ds(pl.multiple_of(n * HISTORY, HISTORY), HISTORY)
        spk_t[:, rows] = spk[rows, :].astype(F32).T.astype(BF16)

    own_first = half_own * 4 + 1

    def features(k):
        block = lax.rem(own_first + k, 8)
        rows = pl.ds(pl.multiple_of(k * HISTORY, HISTORY), HISTORY)
        window = pl.ds(pl.multiple_of(block * HISTORY, HISTORY), 2 * HISTORY)
        made = jnp.dot(lag[...], spk[window, :], preferred_element_type=F32)
        for b in range(BASES):
            x[rows, b * NEUR : (b + 1) * NEUR] = made[b * HISTORY : (b + 1) * HISTORY].astype(BF16)
        made_t = jnp.dot(spk_t[:, window], lag_t[...], preferred_element_type=F32)
        for b in range(BASES):
            piece = made_t[:, b * HISTORY : (b + 1) * HISTORY].astype(BF16)
            xt[:, b, :, rows] = piece.reshape(TM, SLOT, HISTORY)

    loads[1].wait()
    loads[2].wait()
    core_arrival().wait_recv()
    each(0, 4, lambda k: turn_spikes(own_first + k))
    each(0, EARLY, features)

    mate_arrival(0, 0).wait_recv()
    for step, other in spreads:
        spread_copy(step, other).start()

    @pl.when(team == 0)
    def _():
        spk[0:HISTORY, :] = jnp.zeros((HISTORY, NEUR), BF16)

    @pl.when(hands_halo)
    def _():
        halo_first().wait_recv()
        for step, other in spreads:
            halo_spread(step, other).start()

    for n, (dy, c, to) in enumerate(onward):
        direction_arrival(behind(at(dy, c))).wait_recv()
        direction_onward(n).start()

    def predictor(first, last):
        made = jnp.dot(x[first * HISTORY : last * HISTORY, :], wp[...], preferred_element_type=F32)
        made = made.reshape(last - first, NIN, 16, COLS)
        p_own[first:last] = made
        p_send[first:last] = made.astype(BF16)

    def predictor_copy(late, step):
        blocks_of = slice(EARLY, 8) if late else slice(0, EARLY)
        return remote(
            p_send.at[blocks_of, z_peer(step)], p_recv.at[blocks_of, step], p_sem, late * NIN + step, me, z_peer(step)
        )

    predictor(0, EARLY)
    far_first(NIN, lambda step: predictor_copy(0, step).start())

    for dy in (3, 4, -3):
        for c in range(2):
            g_recv[at(dy, c)] = jnp.zeros((SLOT * BASES, COLS), BF16)

    for copy in blocks[1]:
        copy.wait()
    for k in range(GROUP):
        nd_send[k : k + 1, :] = jnp.sum(r32[k] * r32[k], axis=0, keepdims=True)
        nd_send[GROUP + k : GROUP + k + 1, :] = jnp.sum(d32[k] * d32[k], axis=0, keepdims=True)

    def nd_copy(step):
        return remote(nd_send, nd_recv.at[step], nd_sem, step, tm_peer(step), z)

    each(1, TM, lambda step: nd_copy(step).start())

    for step, other in spreads:
        mate_arrival(step, other).wait_recv()

    @pl.when(team > 0)
    def _():
        each(core, NOUT, lambda step: halo_arrival(step).wait_recv())

    each(0, 5, lambda k: turn_spikes(lax.rem(own_first + 4 + k, 9)))
    each(EARLY, 8, features)
    predictor(EARLY, 8)
    far_first(NIN, lambda step: predictor_copy(1, step).start())

    direction_arrival(behind(at(0, 1 - core))).wait_recv()
    for dy, c in ((-2, 1), (2, 0), (3, 0), (3, 1), (-3, 0), (-3, 1), (4, 0), (4, 1)):
        direction_arrival(behind(at(dy, c))).wait_recv()

    def along_copy(half, step):
        blocks_of = slice(half * 4, half * 4 + 4)
        return remote(
            a_send.at[blocks_of, z_peer(step)], a_recv.at[blocks_of, step], a_sem, half * NIN + step, me, z_peer(step)
        )

    for half in range(2):
        made = jnp.dot(
            x[half * 512 : half * 512 + 512, :], d_all[...].reshape(FEAT, COLS), preferred_element_type=F32
        ).reshape(4, NIN, 16, COLS)
        a_own[half * 4 : half * 4 + 4] = made
        a_send[half * 4 : half * 4 + 4] = made.astype(BF16)
        far_first(NIN, lambda step: along_copy(half, step).start())

    each(1, GROUP, lambda step: tick_arrival(step).wait_recv())
    table = jnp.concatenate([ticks[k, 0:2, :] for k in range(GROUP)] + [jnp.zeros((COLS - 8, COLS), F32)], axis=0)
    ticks_t[...] = table.T
    tick_rows = ticks_t[pl.ds(pl.multiple_of(z * 16, 16), 16), :]
    lane = lax.broadcasted_iota(jnp.int32, (16, COLS), 1)

    each(1, TM, lambda step: nd_copy(step).wait_recv())
    cv_send[0:8, :] = nd_send[...] + jnp.sum(nd_recv[1:TM], axis=0)

    for late in range(2):
        each(1, NIN, lambda step: predictor_copy(late, step).wait_recv())

    def weighted_copy(half, slot, step):
        place = wt_all.at[slice(half * 4, half * 4 + 4), slot]
        return remote(place, place, wt_sem, half * NIN + step, me, z_peer(step))

    curvature_part = jnp.zeros((1, COLS), F32)
    for half in range(2):
        each(1, NIN, lambda step: along_copy(half, step).wait_recv())
        for k in range(half * 4, half * 4 + 4):
            p_sum = p_own[k, z]
            a_sum = a_own[k, z]
            for step in range(1, NIN):
                p_sum += p_recv[k, step].astype(F32)
                a_sum += a_recv[k, step].astype(F32)
            scale = jnp.sum(jnp.where(lane == lax.rem(own_first + k, 8), tick_rows, 0.0), axis=1, keepdims=True)
            weighted = ((scale * jnp.exp(p_sum)) * a_sum).astype(BF16)
            wt_all[k, z] = weighted
            curvature_part += jnp.sum(weighted.astype(F32) * a_sum, axis=0, keepdims=True)
        far_first(NIN, lambda step: weighted_copy(half, z, step).start())
    cv_send[8:16, :] = jnp.concatenate([curvature_part, jnp.zeros((7, COLS), F32)], axis=0)

    def cv_copy(step):
        return remote(cv_send, cv_recv.at[step], cv_sem, step, me, z_peer(step))

    each(1, NIN, lambda step: cv_copy(step).start())

    for half in range(2):
        each(1, NIN, lambda step: weighted_copy(half, z_peer(NIN - step), step).wait_recv())

    def gram_to(peer):
        return remote(g_send.at[peer], g_recv.at[me], g_sem, ahead(peer), peer, z)

    def gram_from(peer):
        return remote(g_send.at[0], g_recv.at[peer], g_sem, behind(peer), peer, z)

    far = [(3, 0, 2), (3, 1, 2), (4, 0, 2), (-3, 0, -2), (-3, 1, -2), (-4, 1, -2)]

    def gram_far(n):
        dy, c, by = far[n]
        return remote(g_send.at[at(dy, c)], h_recv.at[n], h_sem, n, at(by, core), z)

    def gram(dy):
        rows = pl.ds(pl.multiple_of(at(dy, 0), 2), 2)
        made = jnp.dot(
            xt[rows].reshape(2 * SLOT * BASES, BINS), wt_all[...].reshape(BINS, COLS), preferred_element_type=F32
        )
        g_send[rows] = made.astype(BF16).reshape(2, SLOT * BASES, COLS)

    each(0, 3, lambda turn: gram(3 + turn))
    for n in (2, 5, 0, 3, 1, 4):
        gram_far(n).start()
    each(1, NIN, lambda step: cv_copy(step).wait_recv())
    cv_sum = cv_send[...] + jnp.sum(cv_recv[1:NIN], axis=0)
    old_norm = cv_sum[0:4, :]
    c2_send[...] = cv_sum[8:16, :]
    c2_recv[me] = cv_sum[8:16, :]

    def c2_copy(step):
        return remote(c2_send, c2_recv.at[me], c2_sem, step, tm_peer(step), z)

    def c2_arrival(step):
        return remote(c2_send, c2_recv.at[tm_peer(TM - step)], c2_sem, step, tm_peer(step), z)

    far_first(TM, lambda step: c2_copy(step).start())
    each(0, 5, lambda turn: gram(turn - 2))
    gram_to(at(2, 1)).start()
    gram_to(at(-2, 0)).start()
    gram_to(at(0, 1 - core)).start()
    g_recv[me] = g_send[me]
    for n in (2, 5, 0, 3, 1, 4):
        dy, c, by = far[n]
        target = at(dy - by, c)
        gram_far(n).wait_recv()
        g_send[target] = (g_send[target].astype(F32) + h_recv[n].astype(F32)).astype(BF16)
        gram_to(target).start()

    each(1, TM, lambda step: c2_arrival(step).wait_recv())
    step_sizes = []
    for k in range(GROUP):
        total = c2_recv[k, 0:1, :]
        for t in range(1, TM // GROUP):
            total += c2_recv[t * GROUP + k, 0:1, :]
        curvature = total / (BINS * (TM // GROUP)) + RIDGE_WEIGHT * cv_sum[4 + k : 5 + k, :]
        step_size = old_norm[k : k + 1, :] / curvature
        step_sizes.append(step_size)
        step_out[:, k * COLS : (k + 1) * COLS] = step_size

    gram_from(at(0, 1 - core)).wait_recv()
    for dy, c in near:
        gram_from(at(dy, c)).wait_recv()
    nn_send[4:8, :] = jnp.zeros((4, COLS), F32)
    for k in range(GROUP):
        total = g_recv[k].astype(F32)
        for t in range(1, TM // GROUP):
            total += g_recv[t * GROUP + k].astype(F32)
        for b in range(BASES):
            g_nat[k, pl.ds(b, SLOT, stride=BASES), :] = total[b * SLOT : (b + 1) * SLOT]
        product = g_nat[k] / (BINS * (TM // GROUP)) + RIDGE_WEIGHT * d32[k]
        new_residual = r32[k] - step_sizes[k] * product
        product_out[:, k * COLS : (k + 1) * COLS] = product
        nn_send[k : k + 1, :] = jnp.sum(new_residual * new_residual, axis=0, keepdims=True)

    def nn_copy(step):
        return remote(nn_send, nn_recv.at[step], nn_sem, step, tm_peer(step), z)

    far_first(TM, lambda step: nn_copy(step).start())
    each(1, TM, lambda step: nn_copy(step).wait_recv())
    nz_send[...] = nn_send[...] + jnp.sum(nn_recv[1:TM], axis=0)

    def nz_copy(step):
        return remote(nz_send, nz_recv.at[step], nz_sem, step, me, z_peer(step))

    far_first(NIN, lambda step: nz_copy(step).start())
    each(1, NIN, lambda step: nz_copy(step).wait_recv())
    new_norm = nz_send[...] + jnp.sum(nz_recv[1:NIN], axis=0)
    for k in range(GROUP):
        ratio = new_norm[k : k + 1, :] / (old_norm[k : k + 1, :] + NORM_EPS)
        ratio_out[:, k * COLS : (k + 1) * COLS] = ratio

    mate_copy().wait_send()
    core_copy().wait_send()
    for step, other in spreads:
        spread_copy(step, other).wait_send()

    @pl.when(sends_halo)
    def _():
        halo_copy(0).wait_send()
        halo_copy(1).wait_send()

    @pl.when(hands_halo)
    def _():
        for step, other in spreads:
            halo_spread(step, other).wait_send()

    each(1, GROUP, lambda step: tick_copy(step).wait_send())
    for dy, c in near:
        direction_copy(ahead(at(dy, c))).wait_send()
    direction_copy(ahead(at(0, 1 - core))).wait_send()
    for n in range(len(onward)):
        direction_onward(n).wait_send()
    for n in range(len(far)):
        gram_far(n).wait_send()
    for dy, c in near:
        gram_to(at(dy, c)).wait_send()
    gram_to(at(0, 1 - core)).wait_send()
    for copy in (nd_copy, c2_copy, nn_copy):
        each(1, TM, lambda step: copy(step).wait_send())
    for copy in (cv_copy, nz_copy):
        each(1, NIN, lambda step: copy(step).wait_send())
    for half in range(2):
        each(1, NIN, lambda step: along_copy(half, step).wait_send())
        each(1, NIN, lambda step: weighted_copy(half, z, step).wait_send())
        each(1, NIN, lambda step: predictor_copy(half, step).wait_send())


def per_device(spikes, exposure, weights, direction, residual, iterate):
    table = lag_table()
    lag = jnp.asarray(table, BF16)
    lag_t = jnp.asarray(np.ascontiguousarray(table.T), BF16)
    rows, columns = direction.shape
    vmem = pl.BlockSpec(memory_space=pltpu.VMEM)
    hbm = pl.BlockSpec(memory_space=pl.ANY)
    pair = lambda n: pltpu.SemaphoreType.DMA((2, n))
    scratch = [
        pltpu.VMEM((OWN, NEUR), jnp.int32),
        pltpu.VMEM((BASES * HISTORY, 2 * HISTORY), BF16),
        pltpu.VMEM((2 * HISTORY, BASES * HISTORY), BF16),
        pltpu.VMEM((GROUP, rows, COLS), F32),
        pltpu.VMEM((GROUP, rows, COLS), F32),
        pltpu.VMEM((FEAT, COLS), BF16),
        pltpu.VMEM((FEAT, COLS), F32),
        pltpu.VMEM((FEAT, COLS), BF16),
        pltpu.VMEM((HISTORY + BINS, NEUR), BF16),
        pltpu.VMEM((NEUR, HISTORY + BINS), BF16),
        pltpu.VMEM((BINS, FEAT), BF16),
        pltpu.VMEM((TM, BASES, SLOT, BINS), BF16),
        pltpu.VMEM((GROUP, BASES, SLOT, COLS), BF16),
        pltpu.VMEM((BASES, NEUR, COLS), BF16),
        pltpu.VMEM((8, NIN, 16, COLS), F32),
        pltpu.VMEM((8, NIN, 16, COLS), BF16),
        pltpu.VMEM((8, NIN, 16, COLS), BF16),
        pltpu.VMEM((8, NIN, 16, COLS), F32),
        pltpu.VMEM((8, NIN, 16, COLS), BF16),
        pltpu.VMEM((8, NIN, 16, COLS), BF16),
        pltpu.VMEM((8, NIN, 16, COLS), BF16),
        pltpu.VMEM((TM, rows, COLS), BF16),
        pltpu.VMEM((TM, rows, COLS), BF16),
        pltpu.VMEM((6, rows, COLS), BF16),
        pltpu.VMEM((GROUP, rows, COLS), F32),
        pltpu.VMEM((GROUP, 8, COLS), F32),
        pltpu.VMEM((COLS, COLS), F32),
        pltpu.VMEM((8, COLS), F32),
        pltpu.VMEM((TM, 8, COLS), F32),
        pltpu.VMEM((16, COLS), F32),
        pltpu.VMEM((NIN, 16, COLS), F32),
        pltpu.VMEM((8, COLS), F32),
        pltpu.VMEM((TM, 8, COLS), F32),
        pltpu.VMEM((8, COLS), F32),
        pltpu.VMEM((TM, 8, COLS), F32),
        pltpu.VMEM((8, COLS), F32),
        pltpu.VMEM((NIN, 8, COLS), F32),
        pltpu.SemaphoreType.DMA((16,)),
        pltpu.SemaphoreType.DMA((6,)),
        pair(9), pair(10), pair(GROUP),
        pair(TM), pair(2 * NIN), pair(2 * NIN), pair(2 * NIN), pair(TM), pair(6),
        pair(TM), pair(NIN), pair(TM), pair(TM), pair(NIN),
    ]
    product, step_size, ratio = pl.pallas_call(
        kernel,
        out_shape=[jax.ShapeDtypeStruct((rows, columns), F32), *[jax.ShapeDtypeStruct((1, columns), F32)] * 2],
        in_specs=[vmem] + [hbm] * 6,
        out_specs=[vmem] * 3,
        scratch_shapes=scratch,
        compiler_params=pltpu.CompilerParams(
            collective_id=0, has_side_effects=True, vmem_limit_bytes=60 * 2**20
        ),
    )(exposure.reshape(2, COLS), spikes, weights, direction, residual, lag, lag_t)
    new_residual = residual - step_size * product
    return iterate + step_size * direction, new_residual, new_residual + ratio * direction


def solution(mesh):
    in_specs = (
        P("tm", "nin"),
        P("tm"),
        P("nin", "nout"),
        P(("nin", "tm"), "nout"),
        P(("nin", "tm"), "nout"),
        P(("nin", "tm"), "nout"),
    )
    out_specs = (P(("nin", "tm"), "nout"), P(("nin", "tm"), "nout"), P(("nin", "tm"), "nout"))
    return jax.shard_map(
        per_device, mesh=mesh, in_specs=in_specs, out_specs=out_specs, check_vma=False
    )
```

```python
import functools
import math

import jax
import jax.numpy as jnp
import numpy as np
from jax import lax
from jax.experimental import pallas as pl
from jax.experimental.pallas import tpu as pltpu
from jax.sharding import PartitionSpec as P

BASES = 8
HISTORY = 128
RIDGE_WEIGHT = 0.05
NORM_EPS = 1e-06
MESH = pl.DeviceIdType.MESH
F32 = jnp.float32
BF16 = jnp.bfloat16

TM = 16
NIN = 8
NOUT = 4
EARLY = 3
GROUP = 4
BINS = 1024
OWN = 256
NEUR = 256
COLS = 128
FEAT = NEUR * BASES
SLOT = NEUR // TM


def basis_table():
    lag_values = np.arange(1, HISTORY + 1, dtype=np.float32)
    warped = np.log(lag_values + np.float32(1.0))
    log_low = math.log(2.0)
    log_high = math.log(HISTORY + 1.0)
    spacing = (log_high - log_low) / (BASES - 1)
    centers = np.float32(log_low) + np.float32(spacing) * np.arange(BASES, dtype=np.float32)
    phases = (warped[:, None] - centers[None, :]) * np.float32(math.pi / (2.0 * spacing))
    phases = np.clip(phases, np.float32(-math.pi), np.float32(math.pi))
    bumps = np.float32(0.5) * (np.float32(1.0) + np.cos(phases))
    bumps = bumps / np.sum(bumps, axis=0, keepdims=True)
    return bumps.astype(np.float32)


def lag_table():
    basis = basis_table()
    lag = np.arange(HISTORY)[:, None] + HISTORY - np.arange(2 * HISTORY)[None, :]
    valid = (lag >= 1) & (lag <= HISTORY)
    table = np.where(valid[None], basis.T[:, np.clip(lag - 1, 0, HISTORY - 1)], np.float32(0.0))
    return table.reshape(BASES * HISTORY, 2 * HISTORY)


def kernel(
    exposure_ref, spikes_hbm, weights_hbm, direction_hbm, residual_hbm, lag_hbm, lag_t_hbm,
    product_out, step_out, ratio_out,
    spikes_in, lag, lag_t, d32, r32, w16, w32, wp, spk, spk_t, x, xt,
    d_send, d_all, p_own, p_send, p_recv, a_own, a_send, a_recv, wt_all, g_send, g_recv, h_recv, g_nat,
    ticks, ticks_t, nd_send, nd_recv, cv_send, cv_recv, c2_send, c2_recv, nn_send, nn_recv, nz_send, nz_recv,
    load_sem, on_sem, spk_sem, halo_sem, tick_sem, d_sem, p_sem, a_sem, wt_sem, g_sem, h_sem, nd_sem, cv_sem, c2_sem, nn_sem, nz_sem,
):
    me = lax.axis_index("tm")
    z = lax.axis_index("nin")
    xo = lax.axis_index("nout")
    team = me // GROUP
    part = lax.rem(me, GROUP)

    def tm_peer(step):
        return lax.rem(me + step, TM)

    def z_peer(step):
        return lax.rem(z + step, NIN)

    def team_peer(step):
        return team * GROUP + lax.rem(part + step, GROUP)

    chip = me // 2
    core = lax.rem(me, 2)
    half_own = lax.rem(chip, 2)
    mate = chip + 1 - 2 * half_own

    def at(dy, c):
        return lax.rem(chip + dy + TM // 2, TM // 2) * 2 + c

    def ahead(peer):
        return lax.rem(peer + TM - me, TM)

    def behind(peer):
        return lax.rem(me + TM - peer, TM)

    def x_peer(step):
        return lax.rem(xo + step, NOUT)

    def swing(turn, middle):
        return middle + (1 - 2 * lax.rem(turn, 2)) * ((turn + 1) // 2)

    def remote(src, dst, sems, slot, tm_index, z_index, x_index=None):
        return pltpu.make_async_remote_copy(
            src_ref=src, dst_ref=dst, send_sem=sems.at[0, slot], recv_sem=sems.at[1, slot],
            device_id=(tm_index, z_index, xo if x_index is None else x_index), device_id_type=MESH,
        )

    def far_first(count, body):
        each(0, count - 1, lambda turn: body(swing(turn, count // 2)))

    def each(first, last, body):
        def run(step, carry):
            body(step)
            return carry

        lax.fori_loop(first, last, run, 0)

    loads = [
        pltpu.make_async_copy(spikes_hbm, spikes_in, load_sem.at[0]),
        pltpu.make_async_copy(lag_hbm, lag, load_sem.at[1]),
        pltpu.make_async_copy(lag_t_hbm, lag_t, load_sem.at[2]),
        pltpu.make_async_copy(
            weights_hbm.at[:, pl.ds(pl.multiple_of(part * COLS, COLS), COLS)], w16, load_sem.at[3]
        ),
    ]
    blocks = [
        [
            pltpu.make_async_copy(source.at[:, k * COLS : (k + 1) * COLS], target.at[k], load_sem.at[4 + 4 * n + k])
            for k in range(GROUP)
        ]
        for n, (source, target) in enumerate(((direction_hbm, d32), (residual_hbm, r32)))
    ]
    for copy in blocks[0] + loads[:1]:
        copy.start()

    barrier = pltpu.get_barrier_semaphore()

    def greet_tm(step):
        pl.semaphore_signal(barrier, inc=1, device_id=(tm_peer(step), z, xo), device_id_type=MESH)

    def greet_z(step):
        pl.semaphore_signal(barrier, inc=1, device_id=(me, z_peer(step), xo), device_id_type=MESH)

    far_first(TM, greet_tm)
    far_first(NIN, greet_z)

    def greet_x(step):
        for c in range(2):
            pl.semaphore_signal(
                barrier, inc=1, device_id=(chip * 2 + c, z, x_peer(step)), device_id_type=MESH
            )

    each(1, NOUT, greet_x)
    for copy in loads[1:] + blocks[1]:
        copy.start()

    for copy in blocks[0]:
        copy.wait()
    for k in range(GROUP):
        for b in range(BASES):
            d_send[k, b] = d32[k, pl.ds(b, SLOT, stride=BASES), :].astype(BF16)
    loads[0].wait()
    own_rows = pl.ds(pl.multiple_of(HISTORY + part * OWN, HISTORY), OWN)
    spk[own_rows, :] = spikes_in[...].astype(F32).astype(BF16)
    ticks[part, 0:2, :] = exposure_ref[...].astype(F32) / 8.0
    ticks[part, 2:8, :] = jnp.zeros((6, COLS), F32)
    pl.semaphore_wait(barrier, TM - 1 + NIN - 1 + 2 * (NOUT - 1))

    def core_copy():
        return remote(spk.at[own_rows], spk.at[own_rows], spk_sem, 8, chip * 2 + 1 - core, z)

    def core_arrival():
        rows = pl.ds(pl.multiple_of(HISTORY + (half_own * 2 + 1 - core) * OWN, HISTORY), OWN)
        return remote(spk.at[rows], spk.at[rows], spk_sem, 8, chip * 2 + 1 - core, z)

    def quarter(half, from_core, x_index):
        return pl.ds(pl.multiple_of(HISTORY + (half * 2 + from_core) * OWN + x_index * 64, 64), 64)

    def mate_copy():
        rows = quarter(half_own, core, xo)
        return remote(spk.at[rows], spk.at[rows], spk_sem, 0, mate * 2 + core, z)

    def mate_arrival(step, other):
        from_core = core if other == 0 else 1 - core
        rows = quarter(1 - half_own, from_core, x_peer(NOUT - step))
        return remote(spk.at[rows], spk.at[rows], spk_sem, step * 2 + other, me, z)

    def spread_copy(step, other):
        rows = quarter(1 - half_own, core, xo)
        to_core = core if other == 0 else 1 - core
        return remote(spk.at[rows], spk.at[rows], spk_sem, step * 2 + other, chip * 2 + to_core, z, x_peer(step))

    def halo_copy(k):
        rows = pl.ds(pl.multiple_of(BINS + xo * 32, 32), 32)
        return remote(
            spk.at[rows], spk.at[halo_rows(xo)], halo_sem, 8 + k, lax.rem((team + 1) * GROUP + 2 * k + 1, TM), z
        )

    def halo_rows(x_index):
        return pl.ds(pl.multiple_of(x_index * 32, 32), 32)

    def halo_first():
        rows = halo_rows(xo)
        return remote(spk.at[rows], spk.at[rows], halo_sem, 8 + half_own, me, z)

    def halo_spread(step, other):
        rows = halo_rows(xo)
        return remote(spk.at[rows], spk.at[rows], halo_sem, step * 2 + other, chip * 2 + 1 - other, z, x_peer(step))

    def halo_arrival(step):
        rows = halo_rows(x_peer(NOUT - step))
        return remote(spk.at[rows], spk.at[rows], halo_sem, step * 2 + 1 - core, me, z)

    def tick_copy(step):
        return remote(ticks.at[part], ticks.at[part], tick_sem, step, team_peer(step), z)

    def tick_arrival(step):
        slot = lax.rem(part + GROUP - step, GROUP)
        return remote(ticks.at[slot], ticks.at[slot], tick_sem, step, team_peer(step), z)

    d_rows = pl.ds(pl.multiple_of(me * SLOT, SLOT), SLOT)

    def direction_copy(step):
        peer = tm_peer(step)
        return remote(d_send.at[lax.rem(peer, GROUP)], d_all.at[:, d_rows, :], d_sem, step, peer, z)

    def direction_arrival(step):
        rows = pl.ds(pl.multiple_of(tm_peer(TM - step) * SLOT, SLOT), SLOT)
        return remote(d_send.at[0], d_all.at[:, rows, :], d_sem, step, tm_peer(step), z)

    onward = [(-1, 0, 2), (1, 0, -2), (-1, 1, 2), (1, 1, -2), (-2, 0, 2), (2, 1, -2)]

    def direction_onward(n):
        dy, c, to = onward[n]
        origin, target = at(dy, c), at(to, core)
        rows = pl.ds(pl.multiple_of(origin * SLOT, SLOT), SLOT)
        return pltpu.make_async_remote_copy(
            src_ref=d_all.at[:, rows, :], dst_ref=d_all.at[:, rows, :], send_sem=on_sem.at[n],
            recv_sem=d_sem.at[1, lax.rem(target + TM - origin, TM)], device_id=(target, z, xo), device_id_type=MESH,
        )

    sends_halo = jnp.logical_and(part == GROUP - 1, team < TM // GROUP - 1)
    hands_halo = jnp.logical_and(core == 1, team > 0)
    spreads = [(step, other) for step in (2, 1, 3, 0) for other in range(2) if (step, other) != (0, 0)]

    mate_copy().start()

    @pl.when(sends_halo)
    def _():
        halo_copy(0).start()
        halo_copy(1).start()

    core_copy().start()
    near = [(dy, c) for dy in (1, -1, 2, -2) for c in range(2)]
    for dy, c in near:
        direction_copy(ahead(at(dy, c))).start()
    direction_copy(ahead(at(0, 1 - core))).start()
    each(1, GROUP, lambda step: tick_copy(step).start())
    d_all[:, d_rows, :] = d_send[part]

    loads[3].wait()
    w32[...] = w16[...].astype(F32)
    for b in range(BASES):
        wp[b * NEUR : (b + 1) * NEUR, :] = w32[pl.ds(b, NEUR, stride=BASES), :].astype(BF16)

    def turn_spikes(n):
        rows = pl.ds(pl.multiple_of(n * HISTORY, HISTORY), HISTORY)
        spk_t[:, rows] = spk[rows, :].astype(F32).T.astype(BF16)

    own_first = half_own * 4 + 1

    def features(k):
        block = lax.rem(own_first + k, 8)
        rows = pl.ds(pl.multiple_of(k * HISTORY, HISTORY), HISTORY)
        window = pl.ds(pl.multiple_of(block * HISTORY, HISTORY), 2 * HISTORY)
        made = jnp.dot(lag[...], spk[window, :], preferred_element_type=F32)
        for b in range(BASES):
            x[rows, b * NEUR : (b + 1) * NEUR] = made[b * HISTORY : (b + 1) * HISTORY].astype(BF16)
        made_t = jnp.dot(spk_t[:, window], lag_t[...], preferred_element_type=F32)
        for b in range(BASES):
            piece = made_t[:, b * HISTORY : (b + 1) * HISTORY].astype(BF16)
            xt[:, b, :, rows] = piece.reshape(TM, SLOT, HISTORY)

    loads[1].wait()
    loads[2].wait()
    mate_arrival(0, 0).wait_recv()
    for step, other in spreads:
        spread_copy(step, other).start()

    @pl.when(team == 0)
    def _():
        spk[0:HISTORY, :] = jnp.zeros((HISTORY, NEUR), BF16)

    @pl.when(hands_halo)
    def _():
        halo_first().wait_recv()
        for step, other in spreads:
            halo_spread(step, other).start()

    core_arrival().wait_recv()
    each(0, 4, lambda k: turn_spikes(own_first + k))
    each(0, EARLY, features)

    for n, (dy, c, to) in enumerate(onward):
        direction_arrival(behind(at(dy, c))).wait_recv()
        direction_onward(n).start()

    def predictor(first, last):
        made = jnp.dot(x[first * HISTORY : last * HISTORY, :], wp[...], preferred_element_type=F32)
        made = made.reshape(last - first, NIN, 16, COLS)
        p_own[first:last] = made
        p_send[first:last] = made.astype(BF16)

    def predictor_copy(late, step):
        blocks_of = slice(EARLY, 8) if late else slice(0, EARLY)
        return remote(
            p_send.at[blocks_of, z_peer(step)], p_recv.at[blocks_of, step], p_sem, late * NIN + step, me, z_peer(step)
        )

    predictor(0, EARLY)
    far_first(NIN, lambda step: predictor_copy(0, step).start())

    for dy in (3, 4, -3):
        for c in range(2):
            g_recv[at(dy, c)] = jnp.zeros((SLOT * BASES, COLS), BF16)

    for copy in blocks[1]:
        copy.wait()
    for k in range(GROUP):
        nd_send[k : k + 1, :] = jnp.sum(r32[k] * r32[k], axis=0, keepdims=True)
        nd_send[GROUP + k : GROUP + k + 1, :] = jnp.sum(d32[k] * d32[k], axis=0, keepdims=True)

    def nd_copy(step):
        return remote(nd_send, nd_recv.at[step], nd_sem, step, tm_peer(step), z)

    each(1, TM, lambda step: nd_copy(step).start())

    for step, other in spreads:
        mate_arrival(step, other).wait_recv()

    @pl.when(team > 0)
    def _():
        each(core, NOUT, lambda step: halo_arrival(step).wait_recv())

    each(0, 5, lambda k: turn_spikes(lax.rem(own_first + 4 + k, 9)))
    each(EARLY, 8, features)
    predictor(EARLY, 8)
    far_first(NIN, lambda step: predictor_copy(1, step).start())

    direction_arrival(behind(at(0, 1 - core))).wait_recv()
    for dy, c in ((-2, 1), (2, 0), (3, 0), (3, 1), (-3, 0), (-3, 1), (4, 0), (4, 1)):
        direction_arrival(behind(at(dy, c))).wait_recv()

    def along_copy(half, step):
        blocks_of = slice(half * 4, half * 4 + 4)
        return remote(
            a_send.at[blocks_of, z_peer(step)], a_recv.at[blocks_of, step], a_sem, half * NIN + step, me, z_peer(step)
        )

    for half in range(2):
        made = jnp.dot(
            x[half * 512 : half * 512 + 512, :], d_all[...].reshape(FEAT, COLS), preferred_element_type=F32
        ).reshape(4, NIN, 16, COLS)
        a_own[half * 4 : half * 4 + 4] = made
        a_send[half * 4 : half * 4 + 4] = made.astype(BF16)
        far_first(NIN, lambda step: along_copy(half, step).start())

    each(1, GROUP, lambda step: tick_arrival(step).wait_recv())
    table = jnp.concatenate([ticks[k, 0:2, :] for k in range(GROUP)] + [jnp.zeros((COLS - 8, COLS), F32)], axis=0)
    ticks_t[...] = table.T
    tick_rows = ticks_t[pl.ds(pl.multiple_of(z * 16, 16), 16), :]
    lane = lax.broadcasted_iota(jnp.int32, (16, COLS), 1)

    each(1, TM, lambda step: nd_copy(step).wait_recv())
    cv_send[0:8, :] = nd_send[...] + jnp.sum(nd_recv[1:TM], axis=0)

    for late in range(2):
        each(1, NIN, lambda step: predictor_copy(late, step).wait_recv())

    def weighted_copy(half, slot, step):
        place = wt_all.at[slice(half * 4, half * 4 + 4), slot]
        return remote(place, place, wt_sem, half * NIN + step, me, z_peer(step))

    curvature_part = jnp.zeros((1, COLS), F32)
    for half in range(2):
        each(1, NIN, lambda step: along_copy(half, step).wait_recv())
        for k in range(half * 4, half * 4 + 4):
            p_sum = p_own[k, z]
            a_sum = a_own[k, z]
            for step in range(1, NIN):
                p_sum += p_recv[k, step].astype(F32)
                a_sum += a_recv[k, step].astype(F32)
            scale = jnp.sum(jnp.where(lane == lax.rem(own_first + k, 8), tick_rows, 0.0), axis=1, keepdims=True)
            weighted = ((scale * jnp.exp(p_sum)) * a_sum).astype(BF16)
            wt_all[k, z] = weighted
            curvature_part += jnp.sum(weighted.astype(F32) * a_sum, axis=0, keepdims=True)
        far_first(NIN, lambda step: weighted_copy(half, z, step).start())
    cv_send[8:16, :] = jnp.concatenate([curvature_part, jnp.zeros((7, COLS), F32)], axis=0)

    def cv_copy(step):
        return remote(cv_send, cv_recv.at[step], cv_sem, step, me, z_peer(step))

    each(1, NIN, lambda step: cv_copy(step).start())

    for half in range(2):
        each(1, NIN, lambda step: weighted_copy(half, z_peer(NIN - step), step).wait_recv())

    def gram_to(peer):
        return remote(g_send.at[peer], g_recv.at[me], g_sem, ahead(peer), peer, z)

    def gram_from(peer):
        return remote(g_send.at[0], g_recv.at[peer], g_sem, behind(peer), peer, z)

    far = [(3, 0, 2), (3, 1, 2), (4, 0, 2), (-3, 0, -2), (-3, 1, -2), (-4, 1, -2)]

    def gram_far(n):
        dy, c, by = far[n]
        return remote(g_send.at[at(dy, c)], h_recv.at[n], h_sem, n, at(by, core), z)

    def gram(dy):
        rows = pl.ds(pl.multiple_of(at(dy, 0), 2), 2)
        made = jnp.dot(
            xt[rows].reshape(2 * SLOT * BASES, BINS), wt_all[...].reshape(BINS, COLS), preferred_element_type=F32
        )
        g_send[rows] = made.astype(BF16).reshape(2, SLOT * BASES, COLS)

    each(0, 3, lambda turn: gram(3 + turn))
    for n in (2, 5, 0, 3, 1, 4):
        gram_far(n).start()
    each(1, NIN, lambda step: cv_copy(step).wait_recv())
    cv_sum = cv_send[...] + jnp.sum(cv_recv[1:NIN], axis=0)
    old_norm = cv_sum[0:4, :]
    c2_send[...] = cv_sum[8:16, :]
    c2_recv[me] = cv_sum[8:16, :]

    def c2_copy(step):
        return remote(c2_send, c2_recv.at[me], c2_sem, step, tm_peer(step), z)

    def c2_arrival(step):
        return remote(c2_send, c2_recv.at[tm_peer(TM - step)], c2_sem, step, tm_peer(step), z)

    far_first(TM, lambda step: c2_copy(step).start())
    each(0, 5, lambda turn: gram(turn - 2))
    gram_to(at(2, 1)).start()
    gram_to(at(-2, 0)).start()
    gram_to(at(0, 1 - core)).start()
    g_recv[me] = g_send[me]
    for n in (2, 5, 0, 3, 1, 4):
        dy, c, by = far[n]
        target = at(dy - by, c)
        gram_far(n).wait_recv()
        g_send[target] = (g_send[target].astype(F32) + h_recv[n].astype(F32)).astype(BF16)
        gram_to(target).start()

    each(1, TM, lambda step: c2_arrival(step).wait_recv())
    step_sizes = []
    for k in range(GROUP):
        total = c2_recv[k, 0:1, :]
        for t in range(1, TM // GROUP):
            total += c2_recv[t * GROUP + k, 0:1, :]
        curvature = total / (BINS * (TM // GROUP)) + RIDGE_WEIGHT * cv_sum[4 + k : 5 + k, :]
        step_size = old_norm[k : k + 1, :] / curvature
        step_sizes.append(step_size)
        step_out[:, k * COLS : (k + 1) * COLS] = step_size

    gram_from(at(0, 1 - core)).wait_recv()
    for dy, c in near:
        gram_from(at(dy, c)).wait_recv()
    nn_send[4:8, :] = jnp.zeros((4, COLS), F32)
    for k in range(GROUP):
        total = g_recv[k].astype(F32)
        for t in range(1, TM // GROUP):
            total += g_recv[t * GROUP + k].astype(F32)
        for b in range(BASES):
            g_nat[k, pl.ds(b, SLOT, stride=BASES), :] = total[b * SLOT : (b + 1) * SLOT]
        product = g_nat[k] / (BINS * (TM // GROUP)) + RIDGE_WEIGHT * d32[k]
        new_residual = r32[k] - step_sizes[k] * product
        product_out[:, k * COLS : (k + 1) * COLS] = product
        nn_send[k : k + 1, :] = jnp.sum(new_residual * new_residual, axis=0, keepdims=True)

    def nn_copy(step):
        return remote(nn_send, nn_recv.at[step], nn_sem, step, tm_peer(step), z)

    far_first(TM, lambda step: nn_copy(step).start())
    each(1, TM, lambda step: nn_copy(step).wait_recv())
    nz_send[...] = nn_send[...] + jnp.sum(nn_recv[1:TM], axis=0)

    def nz_copy(step):
        return remote(nz_send, nz_recv.at[step], nz_sem, step, me, z_peer(step))

    far_first(NIN, lambda step: nz_copy(step).start())
    each(1, NIN, lambda step: nz_copy(step).wait_recv())
    new_norm = nz_send[...] + jnp.sum(nz_recv[1:NIN], axis=0)
    for k in range(GROUP):
        ratio = new_norm[k : k + 1, :] / (old_norm[k : k + 1, :] + NORM_EPS)
        ratio_out[:, k * COLS : (k + 1) * COLS] = ratio

    mate_copy().wait_send()
    core_copy().wait_send()
    for step, other in spreads:
        spread_copy(step, other).wait_send()

    @pl.when(sends_halo)
    def _():
        halo_copy(0).wait_send()
        halo_copy(1).wait_send()

    @pl.when(hands_halo)
    def _():
        for step, other in spreads:
            halo_spread(step, other).wait_send()

    each(1, GROUP, lambda step: tick_copy(step).wait_send())
    for dy, c in near:
        direction_copy(ahead(at(dy, c))).wait_send()
    direction_copy(ahead(at(0, 1 - core))).wait_send()
    for n in range(len(onward)):
        direction_onward(n).wait_send()
    for n in range(len(far)):
        gram_far(n).wait_send()
    for dy, c in near:
        gram_to(at(dy, c)).wait_send()
    gram_to(at(0, 1 - core)).wait_send()
    for copy in (nd_copy, c2_copy, nn_copy):
        each(1, TM, lambda step: copy(step).wait_send())
    for copy in (cv_copy, nz_copy):
        each(1, NIN, lambda step: copy(step).wait_send())
    for half in range(2):
        each(1, NIN, lambda step: along_copy(half, step).wait_send())
        each(1, NIN, lambda step: weighted_copy(half, z, step).wait_send())
        each(1, NIN, lambda step: predictor_copy(half, step).wait_send())


def per_device(spikes, exposure, weights, direction, residual, iterate):
    table = lag_table()
    lag = jnp.asarray(table, BF16)
    lag_t = jnp.asarray(np.ascontiguousarray(table.T), BF16)
    rows, columns = direction.shape
    vmem = pl.BlockSpec(memory_space=pltpu.VMEM)
    hbm = pl.BlockSpec(memory_space=pl.ANY)
    pair = lambda n: pltpu.SemaphoreType.DMA((2, n))
    scratch = [
        pltpu.VMEM((OWN, NEUR), jnp.int32),
        pltpu.VMEM((BASES * HISTORY, 2 * HISTORY), BF16),
        pltpu.VMEM((2 * HISTORY, BASES * HISTORY), BF16),
        pltpu.VMEM((GROUP, rows, COLS), F32),
        pltpu.VMEM((GROUP, rows, COLS), F32),
        pltpu.VMEM((FEAT, COLS), BF16),
        pltpu.VMEM((FEAT, COLS), F32),
        pltpu.VMEM((FEAT, COLS), BF16),
        pltpu.VMEM((HISTORY + BINS, NEUR), BF16),
        pltpu.VMEM((NEUR, HISTORY + BINS), BF16),
        pltpu.VMEM((BINS, FEAT), BF16),
        pltpu.VMEM((TM, BASES, SLOT, BINS), BF16),
        pltpu.VMEM((GROUP, BASES, SLOT, COLS), BF16),
        pltpu.VMEM((BASES, NEUR, COLS), BF16),
        pltpu.VMEM((8, NIN, 16, COLS), F32),
        pltpu.VMEM((8, NIN, 16, COLS), BF16),
        pltpu.VMEM((8, NIN, 16, COLS), BF16),
        pltpu.VMEM((8, NIN, 16, COLS), F32),
        pltpu.VMEM((8, NIN, 16, COLS), BF16),
        pltpu.VMEM((8, NIN, 16, COLS), BF16),
        pltpu.VMEM((8, NIN, 16, COLS), BF16),
        pltpu.VMEM((TM, rows, COLS), BF16),
        pltpu.VMEM((TM, rows, COLS), BF16),
        pltpu.VMEM((6, rows, COLS), BF16),
        pltpu.VMEM((GROUP, rows, COLS), F32),
        pltpu.VMEM((GROUP, 8, COLS), F32),
        pltpu.VMEM((COLS, COLS), F32),
        pltpu.VMEM((8, COLS), F32),
        pltpu.VMEM((TM, 8, COLS), F32),
        pltpu.VMEM((16, COLS), F32),
        pltpu.VMEM((NIN, 16, COLS), F32),
        pltpu.VMEM((8, COLS), F32),
        pltpu.VMEM((TM, 8, COLS), F32),
        pltpu.VMEM((8, COLS), F32),
        pltpu.VMEM((TM, 8, COLS), F32),
        pltpu.VMEM((8, COLS), F32),
        pltpu.VMEM((NIN, 8, COLS), F32),
        pltpu.SemaphoreType.DMA((16,)),
        pltpu.SemaphoreType.DMA((6,)),
        pair(9), pair(10), pair(GROUP),
        pair(TM), pair(2 * NIN), pair(2 * NIN), pair(2 * NIN), pair(TM), pair(6),
        pair(TM), pair(NIN), pair(TM), pair(TM), pair(NIN),
    ]
    product, step_size, ratio = pl.pallas_call(
        kernel,
        out_shape=[jax.ShapeDtypeStruct((rows, columns), F32), *[jax.ShapeDtypeStruct((1, columns), F32)] * 2],
        in_specs=[vmem] + [hbm] * 6,
        out_specs=[vmem] * 3,
        scratch_shapes=scratch,
        compiler_params=pltpu.CompilerParams(
            collective_id=0, has_side_effects=True, vmem_limit_bytes=60 * 2**20
        ),
    )(exposure.reshape(2, COLS), spikes, weights, direction, residual, lag, lag_t)
    new_residual = residual - step_size * product
    return iterate + step_size * direction, new_residual, new_residual + ratio * direction


def solution(mesh):
    in_specs = (
        P("tm", "nin"),
        P("tm"),
        P("nin", "nout"),
        P(("nin", "tm"), "nout"),
        P(("nin", "tm"), "nout"),
        P(("nin", "tm"), "nout"),
    )
    out_specs = (P(("nin", "tm"), "nout"), P(("nin", "tm"), "nout"), P(("nin", "tm"), "nout"))
    return jax.shard_map(
        per_device, mesh=mesh, in_specs=in_specs, out_specs=out_specs, check_vma=False
    )
```
